32 devices in a mesh: dp: 8 (over y, x, core), leaf: 4 (over z).
Axes of the slice: x: 2, y: 2, z: 4, core: 2. Of those that a mesh axis runs over, the one named last changes fastest.
Arguments:
- predict: float32 [100, 262144], P(None, ('dp', 'leaf')), may hold values from -6 to 256
- labels: int32 [262144], P(('dp', 'leaf')), may hold values from 0 to 99
- leaf_ids: int32 [32, 262144], P(None, ('dp', 'leaf')), may hold values from 0 to 63
Outputs:
- new_predict: float32 [100, 262144], P(None, ('dp', 'leaf'))
- leaf_values: float32 [100, 2048], P(None, 'leaf')
The draws below stay inside these ranges and needn't reach their ends.
All inputs are finite; a program needn't handle non-finite values.
Results may differ from the reference program's by a relative error of at most 0.0044.
Values sent between devices are 32-bit elements; how exact they have to be, the bound alone decides.
No kernel may reach another device: no remote copies, remote signals or barrier semaphores. Data moves between devices by JAX's collectives and lax.ppermute only.
A program may use at most 64 MiB of HBM per device.

```python
import jax
import jax.numpy as jnp
from jax import lax

CLASSES = 100
LEAVES = 64
TREES = 32
ROWS = 262144


def draw_predict(key, part):
    base_key = jax.random.fold_in(key, 0)
    return 1.5 * jax.random.truncated_normal(base_key, -4.0, 4.0, (CLASSES, ROWS), jnp.float32)


def place_ends(values, rng, least, top_value):
    extent = values.shape
    spot = [jax.random.randint(jax.random.fold_in(rng, axis), (), 0, extent[axis]) for axis in range(len(extent))]
    values = values.at[tuple(spot)].set(least)
    longest = extent.index(max(extent))
    spot[longest] = (spot[longest] + 1) % extent[longest]
    return values.at[tuple(spot)].set(top_value)


def setup_inputs(seed: int = 0) -> dict:
    arg_keys = jax.random.split(jax.random.key(seed), 4)
    return {
        "predict": draw_predict(jax.random.fold_in(arg_keys[3], 71), 0),
        "labels": place_ends(jax.random.randint(arg_keys[1], (ROWS,), 0, CLASSES), jax.random.fold_in(arg_keys[1], 1), 0, CLASSES - 1).astype(jnp.int32),
        "leaf_ids": place_ends(jax.random.randint(arg_keys[2], (TREES, ROWS), 0, LEAVES), jax.random.fold_in(arg_keys[2], 1), 0, LEAVES - 1).astype(jnp.int32),
    }


step_size = 0.5
ridge_term = 1.0


def gradients(predict, labels):
    row_max = jnp.max(predict, axis=0, keepdims=True)
    exponent = jnp.exp(predict - row_max)
    probability = exponent / jnp.sum(exponent, axis=0, keepdims=True)
    classes = lax.broadcasted_iota(jnp.int32, predict.shape, 0)
    targets = (classes == labels[None, :]).astype(jnp.float32)
    gradient = (probability - targets).astype(jnp.bfloat16)
    hessian = (probability * (1.0 - probability)).astype(jnp.bfloat16)
    return gradient, hessian


def reference(predict, labels, leaf_ids):
    gradient, hessian = gradients(predict, labels)
    stacked = jnp.concatenate([gradient, hessian], axis=0).astype(jnp.float32).T

    def per_tree(tree_leaf):
        return jax.ops.segment_sum(stacked, tree_leaf, num_segments=LEAVES).T

    leaf_sums = lax.map(per_tree, leaf_ids)
    leaf_sums = jnp.transpose(leaf_sums, (1, 0, 2)).reshape(2 * CLASSES, TREES * LEAVES)
    leaf_values = -step_size * leaf_sums[:CLASSES] / (leaf_sums[CLASSES:] + ridge_term)
    value_rows = leaf_values.T
    offsets = (lax.broadcasted_iota(jnp.int32, (TREES, 1), 0) * LEAVES).astype(jnp.int32)
    flat_ids = (leaf_ids + offsets).astype(jnp.int32)

    def add_tree(running, tree_flat):
        return running + jnp.take(value_rows, tree_flat, axis=0), None

    update, unused = lax.scan(add_tree, jnp.zeros((ROWS, CLASSES), jnp.float32), flat_ids)
    return predict + update.T, leaf_values
```

```python
import functools

import jax
import jax.numpy as jnp
import numpy as np
from jax import lax
from jax.experimental import pallas as pl
from jax.experimental.pallas import tpu as pltpu
from jax.sharding import PartitionSpec as P

LEAVES = 64
PAIR = 2 * LEAVES
STEP_SIZE = 0.5
RIDGE_TERM = 1.0
VMEM_LIMIT = 40 * 1024 * 1024
AXES = ("dp", "leaf")


def round_up(value, multiple):
    return -(-value // multiple) * multiple


class Plan:
    def __init__(self, mesh, pairs):
        dp, leaf = mesh.shape["dp"], mesh.shape["leaf"]
        self.devices = dp * leaf
        core = [leaf] if dp > 1 else []
        chip_bits = (dp - 1).bit_length() - len(core)
        low = (chip_bits + 1) // 2
        x_bits = [leaf << (len(core) + b) for b in range(low)]
        y_bits = [leaf << (len(core) + b) for b in range(low, chip_bits)]
        z_bits = [1 << b for b in range((leaf - 1).bit_length())]
        even, odd = [], []
        for b in range(low):
            step = [x_bits[b]] + y_bits[b : b + 1]
            even += step
            odd += step[::-1]
        even += z_bits
        odd += z_bits[::-1]
        self.masks = [core + even, core + odd]
        self.core = core[0] if core else 0
        self.steps = len(self.masks[0])
        self.halvings = 0
        while self.halvings < self.steps and pairs >> (self.halvings + 1) << (self.halvings + 1) == pairs:
            self.halvings += 1
        self.pairs = pairs
        self.final = pairs >> self.halvings

    def mask(self, device, step):
        return self.masks[1 if device & self.core else 0][step]

    def permutation(self, step):
        return [(d, d ^ self.mask(d, step)) for d in range(self.devices)]

    def owned(self, device, slot):
        half = self.pairs
        pair = slot
        for step in range(self.halvings):
            half //= 2
            if device & self.mask(device, step):
                pair ^= half
        return pair


def one_hot(ids_ref, rows, width):
    slot = lax.broadcasted_iota(jnp.int32, (LEAVES, width), 0).astype(jnp.float32).astype(jnp.bfloat16)
    one, zero = jnp.bfloat16(1), jnp.bfloat16(0)
    blocks = []
    for row in rows:
        ids = ids_ref[pl.ds(row, 1), :].astype(jnp.float32).astype(jnp.bfloat16)
        blocks.append(jnp.where(ids == slot, one, zero))
    return jnp.concatenate(blocks, axis=0)


def pair_rows(table_ref, slots):
    rows = []
    for slot in slots:
        first = table_ref[slot] * 2
        rows += [first, first + 1]
    return rows


def groups(slots):
    return [slots[i : i + 2] for i in range(0, len(slots), 2)]


def accumulate(slots, table_ref, ids_ref, stacked, acc):
    width = ids_ref.shape[1]
    done = 0
    for group in groups(slots):
        hot = one_hot(ids_ref, pair_rows(table_ref, group), width)
        acc[pl.ds(done, hot.shape[0]), :] += lax.dot_general(
            hot, stacked, (((1,), (1,)), ((), ())), preferred_element_type=jnp.float32
        )
        done += hot.shape[0]


def write_sums(count, classes, half, acc, out_ref):
    for i in range(count):
        block = acc[pl.ds(i * PAIR, PAIR), :].T
        out_ref[:, pl.ds(2 * i * PAIR, PAIR)] = block[:classes]
        out_ref[:, pl.ds((2 * i + 1) * PAIR, PAIR)] = block[half : half + classes]


def first_kernel(slots, half, table_ref, predict_ref, labels_ref, ids_ref, stacked_ref, out_ref, acc):
    step = pl.program_id(0)

    @pl.when(step == 0)
    def _():
        acc[...] = jnp.zeros_like(acc)

    predict = predict_ref[...]
    classes, width = predict.shape
    row_max = jnp.max(predict, axis=0, keepdims=True)
    exponent = jnp.exp(predict - row_max)
    probability = exponent / jnp.sum(exponent, axis=0, keepdims=True)
    index = lax.broadcasted_iota(jnp.int32, predict.shape, 0)
    targets = jnp.where(index == labels_ref[...], 1.0, 0.0)
    filler = jnp.zeros((half - classes, width), jnp.float32)
    stacked = jnp.concatenate(
        [probability - targets, filler, probability * (1.0 - probability), filler], axis=0
    ).astype(jnp.bfloat16)
    stacked_ref[...] = stacked
    accumulate(slots, table_ref, ids_ref, stacked, acc)

    @pl.when(step == pl.num_programs(0) - 1)
    def _():
        write_sums(len(slots), classes, half, acc, out_ref)


def sums_kernel(slots, half, table_ref, stacked_ref, ids_ref, out_ref, acc):
    step = pl.program_id(0)

    @pl.when(step == 0)
    def _():
        acc[...] = jnp.zeros_like(acc)

    accumulate(slots, table_ref, ids_ref, stacked_ref[...], acc)

    @pl.when(step == pl.num_programs(0) - 1)
    def _():
        write_sums(len(slots), out_ref.shape[0], half, acc, out_ref)


def block_width(rows):
    width = rows
    while width > 2048 and width % 2 == 0:
        width //= 2
    return width


def sums_cost(slots, half, rows):
    return pl.CostEstimate(
        flops=2 * len(slots) * PAIR * rows * 2 * half, bytes_accessed=2 * half * rows * 2, transcendentals=0
    )


def first_sums(table, predict, labels, leaf_ids, slots, half):
    classes, rows = predict.shape
    trees = leaf_ids.shape[0]
    width = block_width(rows)
    return pl.pallas_call(
        functools.partial(first_kernel, slots, half),
        grid_spec=pltpu.PrefetchScalarGridSpec(
            num_scalar_prefetch=1,
            grid=(rows // width,),
            in_specs=[
                pl.BlockSpec((classes, width), lambda i, t: (0, i)),
                pl.BlockSpec((1, width), lambda i, t: (0, i)),
                pl.BlockSpec((trees, width), lambda i, t: (0, i)),
            ],
            out_specs=[
                pl.BlockSpec((2 * half, width), lambda i, t: (0, i)),
                pl.BlockSpec((classes, 2 * PAIR * len(slots)), lambda i, t: (0, 0)),
            ],
            scratch_shapes=[pltpu.VMEM((PAIR * len(slots), 2 * half), jnp.float32)],
        ),
        out_shape=[
            jax.ShapeDtypeStruct((2 * half, rows), jnp.bfloat16),
            jax.ShapeDtypeStruct((classes, 2 * PAIR * len(slots)), jnp.float32),
        ],
        compiler_params=pltpu.CompilerParams(vmem_limit_bytes=VMEM_LIMIT),
        cost_estimate=sums_cost(slots, half, rows),
        name="gradients_and_sums",
    )(table, predict, labels.reshape(1, rows), leaf_ids)


def more_sums(table, stacked, leaf_ids, classes, slots):
    height, rows = stacked.shape
    trees = leaf_ids.shape[0]
    width = block_width(rows)
    return pl.pallas_call(
        functools.partial(sums_kernel, slots, height // 2),
        grid_spec=pltpu.PrefetchScalarGridSpec(
            num_scalar_prefetch=1,
            grid=(rows // width,),
            in_specs=[
                pl.BlockSpec((height, width), lambda i, t: (0, i)),
                pl.BlockSpec((trees, width), lambda i, t: (0, i)),
            ],
            out_specs=pl.BlockSpec((classes, 2 * PAIR * len(slots)), lambda i, t: (0, 0)),
            scratch_shapes=[pltpu.VMEM((PAIR * len(slots), height), jnp.float32)],
        ),
        out_shape=jax.ShapeDtypeStruct((classes, 2 * PAIR * len(slots)), jnp.float32),
        compiler_params=pltpu.CompilerParams(vmem_limit_bytes=VMEM_LIMIT),
        cost_estimate=sums_cost(slots, height // 2, rows),
        name="leaf_sums",
    )(table, stacked, leaf_ids)


def apply_kernel(slots, table_ref, ids_ref, values_ref, carried_ref, out_ref):
    width = ids_ref.shape[1]
    total = carried_ref[...]
    done = 0
    for group in groups(slots):
        hot = one_hot(ids_ref, pair_rows(table_ref, group), width)
        values = values_ref[:, pl.ds(done, hot.shape[0])].astype(jnp.bfloat16)
        total = total + jnp.dot(values, hot, preferred_element_type=jnp.float32)
        done += hot.shape[0]
    out_ref[...] = total


def apply_values(table, leaf_ids, values, carried, slots):
    classes, rows = carried.shape
    trees = leaf_ids.shape[0]
    width = block_width(rows)
    return pl.pallas_call(
        functools.partial(apply_kernel, slots),
        grid_spec=pltpu.PrefetchScalarGridSpec(
            num_scalar_prefetch=1,
            grid=(rows // width,),
            in_specs=[
                pl.BlockSpec((trees, width), lambda i, t: (0, i)),
                pl.BlockSpec(values.shape, lambda i, t: (0, 0)),
                pl.BlockSpec((classes, width), lambda i, t: (0, i)),
            ],
            out_specs=pl.BlockSpec((classes, width), lambda i, t: (0, i)),
        ),
        out_shape=jax.ShapeDtypeStruct((classes, rows), jnp.float32),
        compiler_params=pltpu.CompilerParams(vmem_limit_bytes=VMEM_LIMIT),
        cost_estimate=pl.CostEstimate(
            flops=2 * len(slots) * PAIR * rows * 2 * classes, bytes_accessed=8 * classes * rows, transcendentals=0
        ),
        name="apply_values",
    )(table, leaf_ids, values, carried)


def newton(sums):
    values = []
    for i in range(sums.shape[1] // (2 * PAIR)):
        gradient = sums[:, 2 * i * PAIR : (2 * i + 1) * PAIR]
        hessian = sums[:, (2 * i + 1) * PAIR : (2 * i + 2) * PAIR]
        values.append(-STEP_SIZE * gradient / (hessian + RIDGE_TERM))
    return values[0] if len(values) == 1 else jnp.concatenate(values, axis=1)


def solution(mesh):
    leaf_count = mesh.shape["leaf"]

    def shards(predict, labels, leaf_ids):
        classes = predict.shape[0]
        pairs = leaf_ids.shape[0] // 2
        plan = Plan(mesh, pairs)
        half = round_up(classes, 16)

        rows = []
        for device in range(plan.devices):
            mine = [plan.owned(device, slot) for slot in range(pairs // 2)]
            other = [plan.owned(device ^ plan.core, slot) for slot in range(pairs // 2)]
            row = mine + other
            place = {pair: slot for slot, pair in enumerate(row)}
            per_leaf = pairs // leaf_count
            leaf = device % leaf_count
            rows.append(row + [place[leaf * per_leaf + i] for i in range(per_leaf)])
        table = jnp.asarray(np.array(rows, np.int32))[lax.axis_index(AXES)]

        def exchange(step, value):
            return lax.ppermute(value, AXES, plan.permutation(step))

        def sums(slots):
            return more_sums(table, stacked, leaf_ids, classes, slots)

        h = pairs // 2
        q = h // 2
        stacked, far_other = first_sums(table, predict, labels, leaf_ids, list(range(h + q, 2 * h)), half)
        far_other = exchange(0, far_other)
        far_mine = sums(list(range(q, h)))
        far = exchange(1, far_mine + far_other)
        near_other = exchange(0, sums(list(range(h, h + q))))
        near_mine = sums(list(range(q)))
        held = near_mine + near_other + far
        for step in range(2, plan.steps):
            if step < plan.halvings:
                keep = held.shape[1] // 2
                held = held[:, :keep] + exchange(step, held[:, keep:])
            else:
                held = held + exchange(step, held)
        values = newton(held)
        for step in reversed(range(2, plan.halvings)):
            values = jnp.concatenate([values, exchange(step, values)], axis=1)
        near_values = values
        far_values = exchange(1, near_values)
        mine_values = jnp.concatenate([near_values, far_values], axis=1)
        all_values = jnp.concatenate([mine_values, exchange(0, mine_values)], axis=1)
        new_predict = apply_values(table, leaf_ids, all_values, predict, list(range(pairs)))
        own = [
            lax.dynamic_slice_in_dim(all_values, table[pairs + i] * PAIR, PAIR, 1) for i in range(pairs // leaf_count)
        ]
        return new_predict, jnp.concatenate(own, axis=1)

    return jax.shard_map(
        shards,
        mesh=mesh,
        in_specs=(P(None, AXES), P(AXES), P(None, AXES)),
        out_specs=(P(None, AXES), P(None, "leaf")),
        check_vma=False,
    )
```

```python
import functools

import jax
import jax.numpy as jnp
from jax import lax
from jax.experimental import pallas as pl
from jax.experimental.pallas import tpu as pltpu
from jax.sharding import PartitionSpec as P

LEAVES = 64
PAIR = 2 * LEAVES
STEP_SIZE = 0.5
RIDGE_TERM = 1.0
VMEM_LIMIT = 24 * 1024 * 1024
FIRST_VMEM_LIMIT = 57 * 1024 * 1024
AXES = ("dp", "leaf")
IN_VMEM = pl.BlockSpec(memory_space=pltpu.VMEM)
IN_HBM = pl.BlockSpec(memory_space=pltpu.HBM)


def round_up(value, multiple):
    return -(-value // multiple) * multiple


class Plan:
    def __init__(self, mesh, pairs):
        dp, leaf = mesh.shape["dp"], mesh.shape["leaf"]
        self.leaf = leaf
        self.devices = dp * leaf
        chip_bits = (dp - 1).bit_length() - 1
        low = (chip_bits + 1) // 2
        x_bits = [leaf << (1 + b) for b in range(low)]
        y_bits = [leaf << (1 + b) for b in range(low, chip_bits)]
        z_bits = [1 << b for b in range((leaf - 1).bit_length())]
        even, odd = [], []
        for b in range(low):
            step = [x_bits[b]] + y_bits[b : b + 1]
            even += step
            odd += step[::-1]
        self.core = leaf
        self.masks = [[leaf] + even + z_bits, [leaf] + odd + z_bits[::-1]]
        self.steps = len(self.masks[0])
        self.halvings = 0
        while self.halvings < self.steps and pairs >> (self.halvings + 1) << (self.halvings + 1) == pairs:
            self.halvings += 1
        self.pairs = pairs

    def permutation(self, step):
        return [(d, d ^ self.masks[1 if d & self.core else 0][step]) for d in range(self.devices)]

    def code(self, device, other):
        odd = (device & self.core) != 0
        codes = []
        for masks in self.masks:
            total = jnp.int32(0)
            for step in range(1, self.halvings):
                half = self.pairs >> (step + 1)
                total = total | jnp.where((device & masks[step]) != 0, half, 0)
            codes.append(total)
        top = self.pairs >> 1
        if other:
            return jnp.where(odd, codes[0], codes[1] | top)
        return jnp.where(odd, codes[1] | top, codes[0])


def own_device(plan):
    return lax.axis_index("dp").astype(jnp.int32) * plan.leaf + lax.axis_index("leaf").astype(jnp.int32)


def one_hot(ids_ref, rows, first, width):
    slot = lax.broadcasted_iota(jnp.int32, (LEAVES, width), 0).astype(jnp.float32).astype(jnp.bfloat16)
    one, zero = jnp.bfloat16(1), jnp.bfloat16(0)
    blocks = []
    for row in rows:
        ids = ids_ref[pl.ds(row, 1), pl.ds(first, width)].astype(jnp.float32).astype(jnp.bfloat16)
        blocks.append(jnp.where(ids == slot, one, zero))
    return jnp.concatenate(blocks, axis=0)


def tree_rows(code, slots):
    rows = []
    for slot in slots:
        first = (slot ^ code) * 2
        rows += [first, first + 1]
    return rows


def groups(slots, size):
    return [slots[i : i + size] for i in range(0, len(slots), size)]


def chunk(rows, limit):
    width = rows
    while width > limit and width % 256 == 0:
        width //= 2
    return width


def pair_sums(hot, stacked):
    return lax.dot_general(hot, stacked, (((1,), (1,)), ((), ())), preferred_element_type=jnp.float32)


def write_sums(sums, half, out_ref, first):
    classes = out_ref.shape[0]
    turned = sums.T
    for i in range(turned.shape[1] // PAIR):
        block = turned[:, i * PAIR : (i + 1) * PAIR]
        out_ref[:, pl.ds(2 * (first + i) * PAIR, PAIR)] = block[:classes]
        out_ref[:, pl.ds((2 * (first + i) + 1) * PAIR, PAIR)] = block[half : half + classes]


def first_kernel(plan, slots, half, width, predict_hbm, labels_hbm, ids_hbm, stacked_hbm, out_ref,
                 predict_ref, labels_ref, ids_ref, stacked_ref, sems, out_sems):
    rows = predict_ref.shape[1]
    classes = predict_ref.shape[0]
    count = rows // width
    copies = [
        pltpu.make_async_copy(labels_hbm, labels_ref, sems.at[0]),
        pltpu.make_async_copy(ids_hbm, ids_ref, sems.at[1]),
    ]
    for i in range(count):
        part = pl.ds(i * width, width)
        copies.append(pltpu.make_async_copy(predict_hbm.at[:, part], predict_ref.at[:, part], sems.at[2 + i]))
    copies[0].start()
    copies[2].start()
    copies[1].start()
    for copy in copies[3:]:
        copy.start()
    tree = tree_rows(plan.code(own_device(plan), True), slots)
    copies[0].wait()
    total = None
    writes = []
    for i in range(count):
        copies[2 + i].wait()
        predict = predict_ref[:, i * width : (i + 1) * width]
        row_max = jnp.max(predict, axis=0, keepdims=True)
        exponent = jnp.exp(predict - row_max)
        probability = exponent * (1.0 / jnp.sum(exponent, axis=0, keepdims=True))
        index = lax.broadcasted_iota(jnp.int32, predict.shape, 0)
        targets = jnp.where(index == labels_ref[:, i * width : (i + 1) * width], 1.0, 0.0)
        filler = jnp.zeros((half - classes, width), jnp.float32)
        stacked = jnp.concatenate(
            [probability - targets, filler, probability * (1.0 - probability), filler], axis=0
        ).astype(jnp.bfloat16)
        stacked_ref[:, i * width : (i + 1) * width] = stacked
        part = pl.ds(i * width, width)
        writes.append(pltpu.make_async_copy(stacked_ref.at[:, part], stacked_hbm.at[:, part], out_sems.at[i]))
        writes[-1].start()
        if i == 0:
            copies[1].wait()
        part = pair_sums(one_hot(ids_ref, tree, i * width, width), stacked)
        total = part if total is None else total + part
    write_sums(total, half, out_ref, 0)
    for write in writes:
        write.wait()


def sums_kernel(plan, parts, half, width, stacked_ref, ids_ref, *out_refs):
    device = own_device(plan)
    rows = stacked_ref.shape[1]
    todo = []
    for (slots, other), out_ref in zip(parts, out_refs):
        tree = tree_rows(plan.code(device, other), slots)
        todo += [(tree[2 * i : 2 * i + 2], out_ref, i) for i in range(len(slots))]
    for group in groups(todo, 4):
        tree = [row for item in group for row in item[0]]
        total = None
        for first in range(0, rows, width):
            part = pair_sums(one_hot(ids_ref, tree, first, width), stacked_ref[:, first : first + width])
            total = part if total is None else total + part
        for i, (_, out_ref, place) in enumerate(group):
            write_sums(total[i * PAIR : (i + 1) * PAIR], half, out_ref, place)


def sums_cost(count, half, rows):
    return pl.CostEstimate(
        flops=2 * count * PAIR * rows * 2 * half, bytes_accessed=2 * half * rows * 2, transcendentals=0
    )


def first_sums(plan, predict, labels, leaf_ids, slots, half):
    classes, rows = predict.shape
    width = chunk(rows, 1024)
    return pl.pallas_call(
        functools.partial(first_kernel, plan, slots, half, width),
        in_specs=[IN_HBM, IN_HBM, IN_HBM],
        out_specs=[IN_HBM, IN_VMEM],
        out_shape=[
            jax.ShapeDtypeStruct((2 * half, rows), jnp.bfloat16),
            jax.ShapeDtypeStruct((classes, 2 * PAIR * len(slots)), jnp.float32),
        ],
        scratch_shapes=[
            pltpu.VMEM((classes, rows), jnp.float32),
            pltpu.VMEM((1, rows), jnp.int32),
            pltpu.VMEM(leaf_ids.shape, jnp.int32),
            pltpu.VMEM((2 * half, rows), jnp.bfloat16),
            pltpu.SemaphoreType.DMA((2 + rows // width,)),
            pltpu.SemaphoreType.DMA((rows // width,)),
        ],
        compiler_params=pltpu.CompilerParams(vmem_limit_bytes=FIRST_VMEM_LIMIT),
        cost_estimate=sums_cost(len(slots), half, rows),
        name="gradients_and_sums",
    )(predict, labels.reshape(1, rows), leaf_ids)


def more_sums(plan, stacked, leaf_ids, classes, parts):
    height, rows = stacked.shape
    return pl.pallas_call(
        functools.partial(sums_kernel, plan, parts, height // 2, chunk(rows, 1024)),
        in_specs=[IN_VMEM, IN_VMEM],
        out_specs=[IN_VMEM] * len(parts),
        out_shape=[jax.ShapeDtypeStruct((classes, 2 * PAIR * len(slots)), jnp.float32) for slots, _ in parts],
        compiler_params=pltpu.CompilerParams(vmem_limit_bytes=VMEM_LIMIT),
        cost_estimate=sums_cost(sum(len(slots) for slots, _ in parts), height // 2, rows),
        name="leaf_sums",
    )(stacked, leaf_ids)


def looked_up(plan, parts, value_refs, ids_ref, first, width):
    device = own_device(plan)
    todo = []
    for (slots, other), value_ref in zip(parts, value_refs):
        tree = tree_rows(plan.code(device, other), slots)
        todo += [(tree[2 * i : 2 * i + 2], value_ref, i) for i in range(len(slots))]
    total = None
    for group in groups(todo, 2):
        tree = [row for item in group for row in item[0]]
        hot = one_hot(ids_ref, tree, first, width)
        values = [ref[:, pl.ds(i * PAIR, PAIR)].astype(jnp.bfloat16) for _, ref, i in group]
        values = values[0] if len(values) == 1 else jnp.concatenate(values, axis=1)
        part = jnp.dot(values, hot, preferred_element_type=jnp.float32)
        total = part if total is None else total + part
    return total


def apply_kernel(plan, parts, width, carried, *refs):
    ids_ref, refs = refs[0], refs[1:]
    value_refs, out_ref = refs[: len(parts)], refs[-1]
    for first in range(0, out_ref.shape[1], width):
        part = pl.ds(first, width)
        total = looked_up(plan, parts, value_refs, ids_ref, first, width)
        out_ref[:, part] = refs[len(parts)][:, part] + total if carried else total


def apply_cost(count, classes, rows):
    return pl.CostEstimate(
        flops=2 * count * PAIR * rows * 2 * classes, bytes_accessed=4 * classes * rows, transcendentals=0
    )


def apply_values(plan, leaf_ids, parts, values, update):
    classes, rows = values[0].shape[0], leaf_ids.shape[1]
    carried = update is not None
    operands = (leaf_ids, *values) + ((update,) if carried else ())
    return pl.pallas_call(
        functools.partial(apply_kernel, plan, parts, chunk(rows, 2048), carried),
        in_specs=[IN_VMEM] * len(operands),
        out_specs=IN_VMEM,
        out_shape=jax.ShapeDtypeStruct((classes, rows), jnp.float32),
        input_output_aliases={len(operands) - 1: 0} if carried else {},
        compiler_params=pltpu.CompilerParams(vmem_limit_bytes=VMEM_LIMIT),
        cost_estimate=apply_cost(sum(len(slots) for slots, _ in parts), classes, rows),
        name="apply_values",
    )(*operands)


def last_kernel(plan, parts, pieces, width, *refs):
    ids_ref, update_ref, predict_hbm = refs[:3]
    value_refs = refs[3 : 3 + len(pieces)]
    out_hbm, own_ref, predict_ref, out_ref, table_ref, in_sems, out_sems = refs[3 + len(pieces) :]
    rows = ids_ref.shape[1]
    count = rows // width
    reads, writes = [], []
    for i in range(count):
        part = pl.ds(i * width, width)
        reads.append(pltpu.make_async_copy(predict_hbm.at[:, part], predict_ref.at[:, part], in_sems.at[i]))
        writes.append(pltpu.make_async_copy(out_ref.at[:, part], out_hbm.at[:, part], out_sems.at[i]))
    for read in reads:
        read.start()
    last = [value_refs[pieces.index(piece)] for piece in parts]
    for i in range(count):
        part = pl.ds(i * width, width)
        total = looked_up(plan, parts, last, ids_ref, i * width, width) + update_ref[:, part]
        reads[i].wait()
        out_ref[:, part] = predict_ref[:, part] + total
        writes[i].start()
    device = own_device(plan)
    half = plan.pairs // 2
    for (slots, other), value_ref in zip(pieces, value_refs):
        first = slots[0] + (half if other else 0)
        table_ref[:, pl.ds(first * PAIR, len(slots) * PAIR)] = value_ref[...]
    mine, theirs = plan.code(device, False), plan.code(device, True)
    per_leaf = plan.pairs // plan.leaf
    for i in range(per_leaf):
        pair = lax.axis_index("leaf").astype(jnp.int32) * per_leaf + i
        place = pair ^ mine
        place = jnp.where(place < half, place, (pair ^ theirs) + half)
        own_ref[:, pl.ds(i * PAIR, PAIR)] = table_ref[:, pl.ds(pl.multiple_of(place * PAIR, PAIR), PAIR)]
    for write in writes:
        write.wait()


def finish(plan, leaf_ids, update, predict, parts, pieces, values):
    classes, rows = predict.shape
    width = chunk(rows, 2048)
    return pl.pallas_call(
        functools.partial(last_kernel, plan, parts, pieces, width),
        in_specs=[IN_VMEM, IN_VMEM, IN_HBM] + [IN_VMEM] * len(values),
        out_specs=[IN_HBM, IN_VMEM],
        out_shape=[
            jax.ShapeDtypeStruct((classes, rows), jnp.float32),
            jax.ShapeDtypeStruct((classes, plan.pairs // plan.leaf * PAIR), jnp.float32),
        ],
        scratch_shapes=[
            pltpu.VMEM((classes, rows), jnp.float32),
            pltpu.VMEM((classes, rows), jnp.float32),
            pltpu.VMEM((classes, plan.pairs * PAIR), jnp.float32),
            pltpu.SemaphoreType.DMA((rows // width,)),
            pltpu.SemaphoreType.DMA((rows // width,)),
        ],
        compiler_params=pltpu.CompilerParams(vmem_limit_bytes=VMEM_LIMIT),
        cost_estimate=apply_cost(sum(len(slots) for slots, _ in parts), classes, rows),
        name="apply_last_values",
    )(leaf_ids, update, predict, *values)


def newton(sums):
    values = []
    for i in range(sums.shape[1] // (2 * PAIR)):
        gradient = sums[:, 2 * i * PAIR : (2 * i + 1) * PAIR]
        hessian = sums[:, (2 * i + 1) * PAIR : (2 * i + 2) * PAIR]
        values.append(-STEP_SIZE * gradient / (hessian + RIDGE_TERM))
    return values[0] if len(values) == 1 else jnp.concatenate(values, axis=1)


def after(value, *earlier):
    return lax.optimization_barrier((value, *earlier))[0]


def solution(mesh):
    def shards(predict, labels, leaf_ids):
        classes = predict.shape[0]
        plan = Plan(mesh, leaf_ids.shape[0] // 2)
        half = round_up(classes, 16)

        def exchange(step, value):
            return lax.ppermute(value, AXES, plan.permutation(step))

        h = plan.pairs // 2
        far = list(range(h // 2, h))
        middle = list(range(h // 4, h // 2))
        near = list(range(h // 4))

        stacked, far_other = first_sums(plan, predict, labels, leaf_ids, far, half)
        far_core = exchange(0, far_other)
        (far_own,) = more_sums(plan, stacked, leaf_ids, classes, [(far, False)])
        far_sums = far_own + far_core
        far_moved = exchange(1, far_sums)
        other, middle_own = more_sums(
            plan, after(stacked, far_sums), leaf_ids, classes, [(near + middle, True), (middle, False)]
        )
        rest = exchange(0, other)
        cut = 2 * PAIR * len(near)
        middle_sums = middle_own + rest[:, cut:] + far_moved[:, cut:]
        middle_moved = exchange(2, middle_sums)
        (near_own,) = more_sums(plan, after(stacked, middle_sums), leaf_ids, classes, [(near, False)])
        held = near_own + rest[:, :cut] + far_moved[:, :cut] + middle_moved
        for step in range(3, plan.steps):
            if step < plan.halvings:
                keep = held.shape[1] // 2
                held = held[:, :keep] + exchange(step, held[:, keep:])
            else:
                held = held + exchange(step, held)
        near_values = newton(held)
        for step in reversed(range(3, plan.halvings)):
            near_values = jnp.concatenate([near_values, exchange(step, near_values)], axis=1)

        near_theirs = exchange(0, near_values)
        middle_values = exchange(2, near_values)
        update = apply_values(
            plan, leaf_ids, [(near, False), (near, True)], [near_values, near_theirs], None
        )
        middle_theirs = exchange(0, after(middle_values, update))
        far_values = exchange(1, after(jnp.concatenate([near_values, middle_values], axis=1), update))
        update = apply_values(
            plan, leaf_ids, [(middle, False), (middle, True)], [middle_values, middle_theirs], update
        )
        far_theirs = exchange(0, after(far_values, update))
        update = apply_values(plan, leaf_ids, [(far, False)], [far_values], update)
        pieces = [(near, False), (middle, False), (far, False), (near, True), (middle, True), (far, True)]
        values = [near_values, middle_values, far_values, near_theirs, middle_theirs, far_theirs]
        return tuple(finish(plan, leaf_ids, update, predict, [(far, True)], pieces, values))

    return jax.shard_map(
        shards,
        mesh=mesh,
        in_specs=(P(None, AXES), P(AXES), P(None, AXES)),
        out_specs=(P(None, AXES), P(None, "leaf")),
        check_vma=False,
    )
```

```python
import functools

import jax
import jax.numpy as jnp
from jax import lax
from jax.experimental import pallas as pl
from jax.experimental.pallas import tpu as pltpu
from jax.sharding import PartitionSpec as P

LEAVES = 64
PAIR = 2 * LEAVES
STEP_SIZE = 0.5
RIDGE_TERM = 1.0
VMEM_LIMIT = 24 * 1024 * 1024
FIRST_VMEM_LIMIT = 57 * 1024 * 1024
AXES = ("dp", "leaf")
IN_VMEM = pl.BlockSpec(memory_space=pltpu.VMEM)
IN_HBM = pl.BlockSpec(memory_space=pltpu.HBM)


def round_up(value, multiple):
    return -(-value // multiple) * multiple


class Plan:
    def __init__(self, mesh, pairs):
        dp, leaf = mesh.shape["dp"], mesh.shape["leaf"]
        self.leaf = leaf
        self.devices = dp * leaf
        chip_bits = (dp - 1).bit_length() - 1
        low = (chip_bits + 1) // 2
        x_bits = [leaf << (1 + b) for b in range(low)]
        y_bits = [leaf << (1 + b) for b in range(low, chip_bits)]
        z_bits = [1 << b for b in range((leaf - 1).bit_length())]
        even, odd = [], []
        for b in range(low):
            step = [x_bits[b]] + y_bits[b : b + 1]
            even += step
            odd += step[::-1]
        self.core = leaf
        self.masks = [[leaf] + even + z_bits, [leaf] + odd + z_bits[::-1]]
        self.steps = len(self.masks[0])
        self.halvings = 0
        while self.halvings < self.steps and pairs >> (self.halvings + 1) << (self.halvings + 1) == pairs:
            self.halvings += 1
        self.pairs = pairs

    def permutation(self, *steps):
        pairs = []
        for device in range(self.devices):
            partner = device
            for step in steps:
                partner ^= self.masks[1 if device & self.core else 0][step]
            pairs.append((device, partner))
        return pairs

    def code(self, device, other):
        odd = (device & self.core) != 0
        codes = []
        for masks in self.masks:
            total = jnp.int32(0)
            for step in range(1, self.halvings):
                half = self.pairs >> (step + 1)
                total = total | jnp.where((device & masks[step]) != 0, half, 0)
            codes.append(total)
        top = self.pairs >> 1
        if other:
            return jnp.where(odd, codes[0], codes[1] | top)
        return jnp.where(odd, codes[1] | top, codes[0])


def own_device(plan):
    return lax.axis_index("dp").astype(jnp.int32) * plan.leaf + lax.axis_index("leaf").astype(jnp.int32)


def one_hot(ids_ref, rows, first, width):
    slot = lax.broadcasted_iota(jnp.int32, (LEAVES, width), 0).astype(jnp.float32).astype(jnp.bfloat16)
    one, zero = jnp.bfloat16(1), jnp.bfloat16(0)
    blocks = []
    for row in rows:
        ids = ids_ref[pl.ds(row, 1), pl.ds(first, width)].astype(jnp.float32).astype(jnp.bfloat16)
        blocks.append(jnp.where(ids == slot, one, zero))
    return jnp.concatenate(blocks, axis=0)


def tree_rows(code, slots):
    rows = []
    for slot in slots:
        first = (slot ^ code) * 2
        rows += [first, first + 1]
    return rows


def groups(slots, size):
    return [slots[i : i + size] for i in range(0, len(slots), size)]


def chunk(rows, limit):
    width = rows
    while width > limit and width % 256 == 0:
        width //= 2
    return width


def pair_sums(hot, stacked):
    return lax.dot_general(hot, stacked, (((1,), (1,)), ((), ())), preferred_element_type=jnp.float32)


def write_sums(sums, half, out_ref, first):
    classes = out_ref.shape[0]
    turned = sums.T
    for i in range(turned.shape[1] // PAIR):
        block = turned[:, i * PAIR : (i + 1) * PAIR]
        out_ref[:, pl.ds(2 * (first + i) * PAIR, PAIR)] = block[:classes]
        out_ref[:, pl.ds((2 * (first + i) + 1) * PAIR, PAIR)] = block[half : half + classes]


def first_kernel(plan, slots, half, width, predict_hbm, labels_hbm, ids_hbm, stacked_hbm, out_ref,
                 predict_ref, labels_ref, ids_ref, stacked_ref, sems, out_sems):
    rows = predict_ref.shape[1]
    classes = predict_ref.shape[0]
    count = rows // width
    copies = [
        pltpu.make_async_copy(labels_hbm, labels_ref, sems.at[0]),
        pltpu.make_async_copy(ids_hbm, ids_ref, sems.at[1]),
    ]
    for i in range(count):
        part = pl.ds(i * width, width)
        copies.append(pltpu.make_async_copy(predict_hbm.at[:, part], predict_ref.at[:, part], sems.at[2 + i]))
    copies[2].start()
    copies[0].start()
    for copy in copies[3:]:
        copy.start()
    copies[1].start()
    tree = tree_rows(plan.code(own_device(plan), True), slots)
    copies[0].wait()
    writes = []
    for i in range(count):
        copies[2 + i].wait()
        predict = predict_ref[:, i * width : (i + 1) * width]
        row_max = jnp.max(predict, axis=0, keepdims=True)
        exponent = jnp.exp(predict - row_max)
        probability = exponent * (1.0 / jnp.sum(exponent, axis=0, keepdims=True))
        index = lax.broadcasted_iota(jnp.int32, predict.shape, 0)
        gradient = jnp.where(index == labels_ref[:, i * width : (i + 1) * width], probability - 1.0, probability)
        filler = jnp.zeros((half - classes, width), jnp.float32)
        stacked_ref[:, i * width : (i + 1) * width] = jnp.concatenate(
            [gradient, filler, probability * (1.0 - probability), filler], axis=0
        ).astype(jnp.bfloat16)
        part = pl.ds(i * width, width)
        writes.append(pltpu.make_async_copy(stacked_ref.at[:, part], stacked_hbm.at[:, part], out_sems.at[i]))
        writes[-1].start()
    copies[1].wait()
    total = None
    for i in range(count):
        part = pair_sums(one_hot(ids_ref, tree, i * width, width), stacked_ref[:, i * width : (i + 1) * width])
        total = part if total is None else total + part
    write_sums(total, half, out_ref, 0)
    for write in writes:
        write.wait()


def second_kernel(plan, slots, half, width, stacked_hbm, ids_hbm, out_ref, stacked_ref, ids_ref, sems):
    rows = stacked_ref.shape[1]
    count = rows // width
    copies = [pltpu.make_async_copy(ids_hbm, ids_ref, sems.at[0])]
    for i in range(count):
        part = pl.ds(i * width, width)
        copies.append(pltpu.make_async_copy(stacked_hbm.at[:, part], stacked_ref.at[:, part], sems.at[1 + i]))
    for copy in copies:
        copy.start()
    tree = tree_rows(plan.code(own_device(plan), False), slots)
    copies[0].wait()
    total = None
    for i in range(count):
        copies[1 + i].wait()
        part = pair_sums(one_hot(ids_ref, tree, i * width, width), stacked_ref[:, i * width : (i + 1) * width])
        total = part if total is None else total + part
    write_sums(total, half, out_ref, 0)


def sums_kernel(plan, parts, half, width, stacked_ref, ids_ref, *out_refs):
    device = own_device(plan)
    rows = stacked_ref.shape[1]
    todo = []
    for (slots, other), out_ref in zip(parts, out_refs):
        tree = tree_rows(plan.code(device, other), slots)
        todo += [(tree[2 * i : 2 * i + 2], out_ref, i) for i in range(len(slots))]
    for group in groups(todo, 4):
        tree = [row for item in group for row in item[0]]
        total = None
        for first in range(0, rows, width):
            part = pair_sums(one_hot(ids_ref, tree, first, width), stacked_ref[:, first : first + width])
            total = part if total is None else total + part
        for i, (_, out_ref, place) in enumerate(group):
            write_sums(total[i * PAIR : (i + 1) * PAIR], half, out_ref, place)


def sums_cost(count, half, rows):
    return pl.CostEstimate(
        flops=2 * count * PAIR * rows * 2 * half, bytes_accessed=2 * half * rows * 2, transcendentals=0
    )


def first_sums(plan, predict, labels, leaf_ids, slots, half):
    classes, rows = predict.shape
    width = chunk(rows, 1024)
    return pl.pallas_call(
        functools.partial(first_kernel, plan, slots, half, width),
        in_specs=[IN_HBM, IN_HBM, IN_HBM],
        out_specs=[IN_HBM, IN_VMEM],
        out_shape=[
            jax.ShapeDtypeStruct((2 * half, rows), jnp.bfloat16),
            jax.ShapeDtypeStruct((classes, 2 * PAIR * len(slots)), jnp.float32),
        ],
        scratch_shapes=[
            pltpu.VMEM((classes, rows), jnp.float32),
            pltpu.VMEM((1, rows), jnp.int32),
            pltpu.VMEM(leaf_ids.shape, jnp.int32),
            pltpu.VMEM((2 * half, rows), jnp.bfloat16),
            pltpu.SemaphoreType.DMA((2 + rows // width,)),
            pltpu.SemaphoreType.DMA((rows // width,)),
        ],
        compiler_params=pltpu.CompilerParams(vmem_limit_bytes=FIRST_VMEM_LIMIT),
        cost_estimate=sums_cost(len(slots), half, rows),
        name="gradients_and_sums",
    )(predict, labels.reshape(1, rows), leaf_ids)


def second_sums(plan, stacked, leaf_ids, classes, slots):
    height, rows = stacked.shape
    width = chunk(rows, 2048)
    return pl.pallas_call(
        functools.partial(second_kernel, plan, slots, height // 2, width),
        in_specs=[IN_HBM, IN_HBM],
        out_specs=IN_VMEM,
        out_shape=jax.ShapeDtypeStruct((classes, 2 * PAIR * len(slots)), jnp.float32),
        scratch_shapes=[
            pltpu.VMEM(stacked.shape, stacked.dtype),
            pltpu.VMEM(leaf_ids.shape, jnp.int32),
            pltpu.SemaphoreType.DMA((1 + rows // width,)),
        ],
        compiler_params=pltpu.CompilerParams(vmem_limit_bytes=FIRST_VMEM_LIMIT),
        cost_estimate=sums_cost(len(slots), height // 2, rows),
        name="second_sums",
    )(stacked, leaf_ids)


def more_sums(plan, stacked, leaf_ids, classes, parts):
    height, rows = stacked.shape
    return pl.pallas_call(
        functools.partial(sums_kernel, plan, parts, height // 2, chunk(rows, 1024)),
        in_specs=[IN_VMEM, IN_VMEM],
        out_specs=[IN_VMEM] * len(parts),
        out_shape=[jax.ShapeDtypeStruct((classes, 2 * PAIR * len(slots)), jnp.float32) for slots, _ in parts],
        compiler_params=pltpu.CompilerParams(vmem_limit_bytes=VMEM_LIMIT),
        cost_estimate=sums_cost(sum(len(slots) for slots, _ in parts), height // 2, rows),
        name="leaf_sums",
    )(stacked, leaf_ids)


def looked_up(plan, parts, value_refs, ids_ref, first, width):
    device = own_device(plan)
    todo = []
    for (slots, other), value_ref in zip(parts, value_refs):
        tree = tree_rows(plan.code(device, other), slots)
        todo += [(tree[2 * i : 2 * i + 2], value_ref, i) for i in range(len(slots))]
    total = None
    for group in groups(todo, 2):
        tree = [row for item in group for row in item[0]]
        hot = one_hot(ids_ref, tree, first, width)
        values = [ref[:, pl.ds(i * PAIR, PAIR)].astype(jnp.bfloat16) for _, ref, i in group]
        values = values[0] if len(values) == 1 else jnp.concatenate(values, axis=1)
        part = jnp.dot(values, hot, preferred_element_type=jnp.float32)
        total = part if total is None else total + part
    return total


def apply_kernel(plan, parts, width, carried, *refs):
    ids_ref, refs = refs[0], refs[1:]
    value_refs, out_ref = refs[: len(parts)], refs[-1]
    for first in range(0, out_ref.shape[1], width):
        part = pl.ds(first, width)
        total = looked_up(plan, parts, value_refs, ids_ref, first, width)
        out_ref[:, part] = refs[len(parts)][:, part] + total if carried else total


def apply_cost(count, classes, rows):
    return pl.CostEstimate(
        flops=2 * count * PAIR * rows * 2 * classes, bytes_accessed=4 * classes * rows, transcendentals=0
    )


def apply_values(plan, leaf_ids, parts, values, update):
    classes, rows = values[0].shape[0], leaf_ids.shape[1]
    carried = update is not None
    operands = (leaf_ids, *values) + ((update,) if carried else ())
    return pl.pallas_call(
        functools.partial(apply_kernel, plan, parts, chunk(rows, 2048), carried),
        in_specs=[IN_VMEM] * len(operands),
        out_specs=IN_VMEM,
        out_shape=jax.ShapeDtypeStruct((classes, rows), jnp.float32),
        input_output_aliases={len(operands) - 1: 0} if carried else {},
        compiler_params=pltpu.CompilerParams(vmem_limit_bytes=VMEM_LIMIT),
        cost_estimate=apply_cost(sum(len(slots) for slots, _ in parts), classes, rows),
        name="apply_values",
    )(*operands)


def last_kernel(plan, parts, pieces, width, *refs):
    ids_ref, update_ref, predict_ref = refs[:3]
    value_refs = refs[3 : 3 + len(pieces)]
    out_hbm, own_hbm, out_ref, own_ref, table_ref, sems = refs[3 + len(pieces) :]
    rows = ids_ref.shape[1]
    count = rows // width
    device = own_device(plan)
    half = plan.pairs // 2
    for (slots, other), value_ref in zip(pieces, value_refs):
        first = slots[0] + (half if other else 0)
        table_ref[:, pl.ds(first * PAIR, len(slots) * PAIR)] = value_ref[...]
    mine, theirs = plan.code(device, False), plan.code(device, True)
    per_leaf = plan.pairs // plan.leaf
    for i in range(per_leaf):
        pair = lax.axis_index("leaf").astype(jnp.int32) * per_leaf + i
        place = pair ^ mine
        place = jnp.where(place < half, place, (pair ^ theirs) + half)
        own_ref[:, pl.ds(i * PAIR, PAIR)] = table_ref[:, pl.ds(pl.multiple_of(place * PAIR, PAIR), PAIR)]
    writes = [pltpu.make_async_copy(own_ref, own_hbm, sems.at[count])]
    writes[0].start()
    last = [value_refs[pieces.index(piece)] for piece in parts]
    for i in range(count):
        part = pl.ds(i * width, width)
        total = looked_up(plan, parts, last, ids_ref, i * width, width) + update_ref[:, part]
        out_ref[:, part] = predict_ref[:, part] + total
        writes.append(pltpu.make_async_copy(out_ref.at[:, part], out_hbm.at[:, part], sems.at[i]))
        writes[-1].start()
    for write in writes:
        write.wait()


def finish(plan, leaf_ids, update, predict, parts, pieces, values):
    classes, rows = predict.shape
    width = chunk(rows, 2048)
    own = (classes, plan.pairs // plan.leaf * PAIR)
    return pl.pallas_call(
        functools.partial(last_kernel, plan, parts, pieces, width),
        in_specs=[IN_VMEM] * (3 + len(values)),
        out_specs=[IN_HBM, IN_HBM],
        out_shape=[jax.ShapeDtypeStruct((classes, rows), jnp.float32), jax.ShapeDtypeStruct(own, jnp.float32)],
        scratch_shapes=[
            pltpu.VMEM((classes, rows), jnp.float32),
            pltpu.VMEM(own, jnp.float32),
            pltpu.VMEM((classes, plan.pairs * PAIR), jnp.float32),
            pltpu.SemaphoreType.DMA((rows // width + 1,)),
        ],
        compiler_params=pltpu.CompilerParams(vmem_limit_bytes=VMEM_LIMIT),
        cost_estimate=apply_cost(sum(len(slots) for slots, _ in parts), classes, rows),
        name="apply_last_values",
    )(leaf_ids, update, predict, *values)


def newton(sums):
    values = []
    for i in range(sums.shape[1] // (2 * PAIR)):
        gradient = sums[:, 2 * i * PAIR : (2 * i + 1) * PAIR]
        hessian = sums[:, (2 * i + 1) * PAIR : (2 * i + 2) * PAIR]
        values.append(-STEP_SIZE * gradient / (hessian + RIDGE_TERM))
    return values[0] if len(values) == 1 else jnp.concatenate(values, axis=1)


def after(value, *earlier):
    return lax.optimization_barrier((value, *earlier))[0]


def solution(mesh):
    def shards(predict, labels, leaf_ids):
        classes = predict.shape[0]
        plan = Plan(mesh, leaf_ids.shape[0] // 2)
        half = round_up(classes, 16)

        def exchange(value, *steps):
            return lax.ppermute(value, AXES, plan.permutation(*steps))

        h = plan.pairs // 2
        far = list(range(h // 2, h))
        middle = list(range(h // 4, h // 2))
        near = list(range(h // 4))

        stacked, far_other = first_sums(plan, predict, labels, leaf_ids, far, half)
        far_core = exchange(far_other, 0)
        far_own = second_sums(plan, stacked, leaf_ids, classes, far)
        far_sums = far_own + far_core
        far_moved = exchange(far_sums, 1)
        other, middle_own = more_sums(
            plan, after(stacked, far_sums), leaf_ids, classes, [(near + middle, True), (middle, False)]
        )
        rest = exchange(other, 0)
        cut = 2 * PAIR * len(near)
        middle_sums = middle_own + rest[:, cut:] + far_moved[:, cut:]
        middle_moved = exchange(middle_sums, 2)
        (near_own,) = more_sums(plan, after(stacked, middle_sums), leaf_ids, classes, [(near, False)])
        held = near_own + rest[:, :cut] + far_moved[:, :cut] + middle_moved
        for step in range(3, plan.steps):
            if step < plan.halvings:
                keep = held.shape[1] // 2
                held = held[:, :keep] + exchange(held[:, keep:], step)
            else:
                held = held + exchange(held, step)
        near_values = newton(held)
        for step in reversed(range(3, plan.halvings)):
            near_values = jnp.concatenate([near_values, exchange(near_values, step)], axis=1)

        near_theirs = exchange(near_values, 0)
        both_values = exchange(near_values, 1, 2)
        first_values = exchange(near_values, 1)
        second_values = exchange(near_values, 2)

        def apply(parts, values, update):
            return apply_values(plan, leaf_ids, parts, values, update)

        first = list(range(h // 2, h // 2 + len(near)))
        both = list(range(h // 2 + len(near), h))
        update = apply([(near, False), (near, True)], [near_values, near_theirs], None)
        both_theirs = exchange(after(both_values, update), 0)
        first_theirs = exchange(after(first_values, update), 0)
        update = apply([(both, False), (both, True)], [both_values, both_theirs], update)
        second_theirs = exchange(after(second_values, update), 0)
        update = apply([(first, False), (first, True)], [first_values, first_theirs], update)
        pieces = [(slots, other) for other in (False, True) for slots in (near, middle, first, both)]
        values = [near_values, second_values, first_values, both_values]
        values += [near_theirs, second_theirs, first_theirs, both_theirs]
        last = [(middle, False), (middle, True)]
        return tuple(finish(plan, leaf_ids, update, predict, last, pieces, values))

    return jax.shard_map(
        shards,
        mesh=mesh,
        in_specs=(P(None, AXES), P(AXES), P(None, AXES)),
        out_specs=(P(None, AXES), P(None, "leaf")),
        check_vma=False,
    )
```

```python
import functools

import jax
import jax.numpy as jnp
from jax import lax
from jax.experimental import pallas as pl
from jax.experimental.pallas import tpu as pltpu
from jax.sharding import PartitionSpec as P

LEAVES = 64
PAIR = 2 * LEAVES
STEP_SIZE = 0.5
RIDGE_TERM = 1.0
VMEM_LIMIT = 24 * 1024 * 1024
AXES = ("dp", "leaf")
IN_VMEM = pl.BlockSpec(memory_space=pltpu.VMEM)
IN_HBM = pl.BlockSpec(memory_space=pltpu.HBM)


def round_up(value, multiple):
    return -(-value // multiple) * multiple


class Plan:
    def __init__(self, mesh, pairs):
        dp, leaf = mesh.shape["dp"], mesh.shape["leaf"]
        self.leaf = leaf
        self.devices = dp * leaf
        chip_bits = (dp - 1).bit_length() - 1
        low = (chip_bits + 1) // 2
        x_bits = [leaf << (1 + b) for b in range(low)]
        y_bits = [leaf << (1 + b) for b in range(low, chip_bits)]
        z_bits = [1 << b for b in range((leaf - 1).bit_length())]
        even, odd = [], []
        for b in range(low):
            step = [x_bits[b]] + y_bits[b : b + 1]
            even += step
            odd += step[::-1]
        self.core = leaf
        self.masks = [[leaf] + even + z_bits, [leaf] + odd + z_bits[::-1]]
        self.steps = len(self.masks[0])
        self.halvings = 0
        while self.halvings < self.steps and pairs >> (self.halvings + 1) << (self.halvings + 1) == pairs:
            self.halvings += 1
        self.pairs = pairs

    def permutation(self, *steps):
        pairs = []
        for device in range(self.devices):
            partner = device
            for step in steps:
                partner ^= self.masks[1 if device & self.core else 0][step]
            pairs.append((device, partner))
        return pairs

    def code(self, device, other):
        odd = (device & self.core) != 0
        codes = []
        for masks in self.masks:
            total = jnp.int32(0)
            for step in range(1, self.halvings):
                half = self.pairs >> (step + 1)
                total = total | jnp.where((device & masks[step]) != 0, half, 0)
            codes.append(total)
        top = self.pairs >> 1
        if other:
            return jnp.where(odd, codes[0], codes[1] | top)
        return jnp.where(odd, codes[1] | top, codes[0])


def own_device(plan):
    return lax.axis_index("dp").astype(jnp.int32) * plan.leaf + lax.axis_index("leaf").astype(jnp.int32)


def one_hot(ids_ref, rows, first, width):
    slot = lax.broadcasted_iota(jnp.int32, (LEAVES, width), 0).astype(jnp.float32).astype(jnp.bfloat16)
    one, zero = jnp.bfloat16(1), jnp.bfloat16(0)
    blocks = []
    for row in rows:
        ids = ids_ref[pl.ds(row, 1), pl.ds(first, width)].astype(jnp.float32).astype(jnp.bfloat16)
        blocks.append(jnp.where(ids == slot, one, zero))
    return jnp.concatenate(blocks, axis=0)


def tree_rows(code, slots):
    rows = []
    for slot in slots:
        first = (slot ^ code) * 2
        rows += [first, first + 1]
    return rows


def groups(slots, size):
    return [slots[i : i + size] for i in range(0, len(slots), size)]


def chunk(rows, limit):
    width = rows
    while width > limit and width % 256 == 0:
        width //= 2
    return width


def pair_sums(hot, stacked):
    return lax.dot_general(hot, stacked, (((1,), (1,)), ((), ())), preferred_element_type=jnp.float32)


def write_sums(sums, half, out_ref, first):
    classes = out_ref.shape[0]
    turned = sums.T
    for i in range(turned.shape[1] // PAIR):
        block = turned[:, i * PAIR : (i + 1) * PAIR]
        out_ref[:, pl.ds(2 * (first + i) * PAIR, PAIR)] = block[:classes]
        out_ref[:, pl.ds((2 * (first + i) + 1) * PAIR, PAIR)] = block[half : half + classes]


def add_up(plan, parts, half, width, stacked_ref, ids_ref, out_refs):
    device = own_device(plan)
    rows = stacked_ref.shape[1]
    todo = []
    for (slots, other), out_ref in zip(parts, out_refs):
        tree = tree_rows(plan.code(device, other), slots)
        todo += [(tree[2 * i : 2 * i + 2], out_ref, i) for i in range(len(slots))]
    for group in groups(todo, 4):
        tree = [row for item in group for row in item[0]]
        total = None
        for first in range(0, rows, width):
            part = pair_sums(one_hot(ids_ref, tree, first, width), stacked_ref[:, first : first + width])
            total = part if total is None else total + part
        for i, (_, out_ref, place) in enumerate(group):
            write_sums(total[i * PAIR : (i + 1) * PAIR], half, out_ref, place)


def first_kernel(plan, slots, half, width, predict_hbm, labels_hbm, ids_hbm, stacked_ref, other_ref,
                 predict_ref, labels_ref, ids_ref, sems):
    rows = predict_ref.shape[1]
    classes = predict_ref.shape[0]
    count = rows // width
    copies = [
        pltpu.make_async_copy(labels_hbm, labels_ref, sems.at[0]),
        pltpu.make_async_copy(ids_hbm, ids_ref, sems.at[1]),
    ]
    for i in range(count):
        part = pl.ds(i * width, width)
        copies.append(pltpu.make_async_copy(predict_hbm.at[:, part], predict_ref.at[:, part], sems.at[2 + i]))
    copies[2].start()
    copies[0].start()
    for copy in copies[3:]:
        copy.start()
    copies[1].start()
    copies[0].wait()
    for i in range(count):
        copies[2 + i].wait()
        predict = predict_ref[:, i * width : (i + 1) * width]
        row_max = jnp.max(predict, axis=0, keepdims=True)
        exponent = jnp.exp(predict - row_max)
        probability = exponent * (1.0 / jnp.sum(exponent, axis=0, keepdims=True))
        index = lax.broadcasted_iota(jnp.int32, predict.shape, 0)
        gradient = jnp.where(index == labels_ref[:, i * width : (i + 1) * width], probability - 1.0, probability)
        filler = jnp.zeros((half - classes, width), jnp.float32)
        stacked_ref[:, i * width : (i + 1) * width] = jnp.concatenate(
            [gradient, filler, probability * (1.0 - probability), filler], axis=0
        ).astype(jnp.bfloat16)
    copies[1].wait()
    add_up(plan, [(slots, True)], half, width, stacked_ref, ids_ref, (other_ref,))


def sums_kernel(plan, parts, half, width, stacked_ref, ids_ref, _, *out_refs):
    add_up(plan, parts, half, width, stacked_ref, ids_ref, out_refs)


def sums_cost(count, half, rows):
    return pl.CostEstimate(
        flops=2 * count * PAIR * rows * 2 * half, bytes_accessed=2 * half * rows * 2, transcendentals=0
    )


def first_sums(plan, predict, labels, leaf_ids, slots, half):
    classes, rows = predict.shape
    width = chunk(rows, 1024)
    return pl.pallas_call(
        functools.partial(first_kernel, plan, slots, half, width),
        in_specs=[IN_HBM, IN_HBM, IN_HBM],
        out_specs=[IN_VMEM, IN_VMEM],
        out_shape=[
            pltpu.VMEM((2 * half, rows), jnp.bfloat16),
            pltpu.VMEM((classes, 2 * PAIR * len(slots)), jnp.float32),
        ],
        scratch_shapes=[
            pltpu.VMEM((classes, rows), jnp.float32),
            pltpu.VMEM((1, rows), jnp.int32),
            pltpu.VMEM(leaf_ids.shape, jnp.int32),
            pltpu.SemaphoreType.DMA((2 + rows // width,)),
        ],
        compiler_params=pltpu.CompilerParams(vmem_limit_bytes=VMEM_LIMIT),
        cost_estimate=sums_cost(len(slots), half, rows),
        name="gradients_and_sums",
    )(*(pltpu.with_memory_space_constraint(x, pltpu.HBM) for x in (predict, labels.reshape(1, rows), leaf_ids)))


def more_sums(plan, stacked, leaf_ids, classes, parts, earlier):
    height, rows = stacked.shape
    return pl.pallas_call(
        functools.partial(sums_kernel, plan, parts, height // 2, chunk(rows, 1024)),
        in_specs=[IN_VMEM, IN_VMEM, pl.BlockSpec(memory_space=pl.ANY)],
        out_specs=[IN_VMEM] * len(parts),
        out_shape=[jax.ShapeDtypeStruct((classes, 2 * PAIR * len(slots)), jnp.float32) for slots, _ in parts],
        compiler_params=pltpu.CompilerParams(vmem_limit_bytes=VMEM_LIMIT),
        cost_estimate=sums_cost(sum(len(slots) for slots, _ in parts), height // 2, rows),
        name="leaf_sums",
    )(stacked, leaf_ids, earlier)


def looked_up(plan, parts, value_refs, ids_ref, first, width):
    device = own_device(plan)
    todo = []
    for (slots, other), value_ref in zip(parts, value_refs):
        tree = tree_rows(plan.code(device, other), slots)
        todo += [(tree[2 * i : 2 * i + 2], value_ref, i) for i in range(len(slots))]
    total = None
    for group in groups(todo, 2):
        tree = [row for item in group for row in item[0]]
        hot = one_hot(ids_ref, tree, first, width)
        values = [ref[:, pl.ds(i * PAIR, PAIR)].astype(jnp.bfloat16) for _, ref, i in group]
        values = values[0] if len(values) == 1 else jnp.concatenate(values, axis=1)
        part = jnp.dot(values, hot, preferred_element_type=jnp.float32)
        total = part if total is None else total + part
    return total


def apply_kernel(plan, parts, width, carried, *refs):
    ids_ref, refs = refs[0], refs[1:]
    value_refs, out_ref = refs[: len(parts)], refs[-1]
    for first in range(0, out_ref.shape[1], width):
        part = pl.ds(first, width)
        total = looked_up(plan, parts, value_refs, ids_ref, first, width)
        out_ref[:, part] = refs[len(parts)][:, part] + total if carried else total


def apply_cost(count, classes, rows):
    return pl.CostEstimate(
        flops=2 * count * PAIR * rows * 2 * classes, bytes_accessed=4 * classes * rows, transcendentals=0
    )


def apply_values(plan, leaf_ids, parts, values, update):
    classes, rows = values[0].shape[0], leaf_ids.shape[1]
    carried = update is not None
    operands = (leaf_ids, *values) + ((update,) if carried else ())
    return pl.pallas_call(
        functools.partial(apply_kernel, plan, parts, chunk(rows, 2048), carried),
        in_specs=[IN_VMEM] * len(operands),
        out_specs=IN_VMEM,
        out_shape=jax.ShapeDtypeStruct((classes, rows), jnp.float32),
        input_output_aliases={len(operands) - 1: 0} if carried else {},
        compiler_params=pltpu.CompilerParams(vmem_limit_bytes=VMEM_LIMIT),
        cost_estimate=apply_cost(sum(len(slots) for slots, _ in parts), classes, rows),
        name="apply_values",
    )(*operands)


def last_kernel(plan, parts, pieces, width, *refs):
    ids_ref, update_ref, predict_ref = refs[:3]
    value_refs = refs[3 : 3 + len(pieces)]
    out_hbm, own_hbm, out_ref, own_ref, table_ref, sems = refs[3 + len(pieces) :]
    rows = ids_ref.shape[1]
    count = rows // width
    device = own_device(plan)
    half = plan.pairs // 2
    for (slots, other), value_ref in zip(pieces, value_refs):
        first = slots[0] + (half if other else 0)
        table_ref[:, pl.ds(first * PAIR, len(slots) * PAIR)] = value_ref[...]
    mine, theirs = plan.code(device, False), plan.code(device, True)
    per_leaf = plan.pairs // plan.leaf
    for i in range(per_leaf):
        pair = lax.axis_index("leaf").astype(jnp.int32) * per_leaf + i
        place = pair ^ mine
        place = jnp.where(place < half, place, (pair ^ theirs) + half)
        own_ref[:, pl.ds(i * PAIR, PAIR)] = table_ref[:, pl.ds(pl.multiple_of(place * PAIR, PAIR), PAIR)]
    writes = [pltpu.make_async_copy(own_ref, own_hbm, sems.at[count])]
    writes[0].start()
    last = [value_refs[pieces.index(piece)] for piece in parts]
    for i in range(count):
        part = pl.ds(i * width, width)
        total = looked_up(plan, parts, last, ids_ref, i * width, width) + update_ref[:, part]
        out_ref[:, part] = predict_ref[:, part] + total
        writes.append(pltpu.make_async_copy(out_ref.at[:, part], out_hbm.at[:, part], sems.at[i]))
        writes[-1].start()
    for write in writes:
        write.wait()


def finish(plan, leaf_ids, update, predict, parts, pieces, values):
    classes, rows = predict.shape
    width = chunk(rows, 2048)
    own = (classes, plan.pairs // plan.leaf * PAIR)
    return pl.pallas_call(
        functools.partial(last_kernel, plan, parts, pieces, width),
        in_specs=[IN_VMEM] * (3 + len(values)),
        out_specs=[IN_HBM, IN_HBM],
        out_shape=[jax.ShapeDtypeStruct((classes, rows), jnp.float32), jax.ShapeDtypeStruct(own, jnp.float32)],
        scratch_shapes=[
            pltpu.VMEM((classes, rows), jnp.float32),
            pltpu.VMEM(own, jnp.float32),
            pltpu.VMEM((classes, plan.pairs * PAIR), jnp.float32),
            pltpu.SemaphoreType.DMA((rows // width + 1,)),
        ],
        compiler_params=pltpu.CompilerParams(vmem_limit_bytes=VMEM_LIMIT),
        cost_estimate=apply_cost(sum(len(slots) for slots, _ in parts), classes, rows),
        name="apply_last_values",
    )(leaf_ids, update, predict, *values)


def newton(sums):
    values = []
    for i in range(sums.shape[1] // (2 * PAIR)):
        gradient = sums[:, 2 * i * PAIR : (2 * i + 1) * PAIR]
        hessian = sums[:, (2 * i + 1) * PAIR : (2 * i + 2) * PAIR]
        values.append(-STEP_SIZE * gradient / (hessian + RIDGE_TERM))
    return values[0] if len(values) == 1 else jnp.concatenate(values, axis=1)


def solution(mesh):
    def shards(predict, labels, leaf_ids):
        classes = predict.shape[0]
        plan = Plan(mesh, leaf_ids.shape[0] // 2)
        half = round_up(classes, 16)

        def exchange(value, *steps):
            return lax.ppermute(value, AXES, plan.permutation(*steps))

        h = plan.pairs // 2
        far = list(range(h // 2, h))
        middle = list(range(h // 4, h // 2))
        near = list(range(h // 4))

        stacked, far_other = first_sums(plan, predict, labels, leaf_ids, far, half)
        (far_own,) = more_sums(plan, stacked, leaf_ids, classes, [(far, False)], far_other)
        far_sums = far_own + exchange(far_other, 0)
        far_moved = exchange(far_sums, 1)
        other, middle_own = more_sums(
            plan, stacked, leaf_ids, classes, [(near + middle, True), (middle, False)], far_sums
        )
        rest = exchange(other, 0)
        cut = 2 * PAIR * len(near)
        middle_sums = middle_own + rest[:, cut:] + far_moved[:, cut:]
        middle_moved = exchange(middle_sums, 2)
        (near_own,) = more_sums(plan, stacked, leaf_ids, classes, [(near, False)], middle_sums)
        held = near_own + rest[:, :cut] + far_moved[:, :cut] + middle_moved
        for step in range(3, plan.steps):
            if step < plan.halvings:
                keep = held.shape[1] // 2
                held = held[:, :keep] + exchange(held[:, keep:], step)
            else:
                held = held + exchange(held, step)
        near_values = newton(held)
        for step in reversed(range(3, plan.halvings)):
            near_values = jnp.concatenate([near_values, exchange(near_values, step)], axis=1)

        near_theirs = exchange(near_values, 0)
        both_values = exchange(near_values, 1, 2)
        first_values = exchange(near_values, 1)
        second_values = exchange(near_values, 2)

        def apply(parts, values, update):
            return apply_values(plan, leaf_ids, parts, values, update)

        first = list(range(h // 2, h // 2 + len(near)))
        both = list(range(h // 2 + len(near), h))
        update = apply([(near, False), (near, True)], [near_values, near_theirs], None)
        update, both_values, first_values, second_values = lax.optimization_barrier(
            (update, both_values, first_values, second_values)
        )
        both_theirs = exchange(both_values, 0)
        first_theirs = exchange(first_values, 0)
        second_theirs = exchange(second_values, 0)
        update = apply([(both, False), (first, False)], [both_values, first_values], update)
        pieces = [(slots, other) for other in (False, True) for slots in (near, middle, first, both)]
        values = [near_values, second_values, first_values, both_values]
        values += [near_theirs, second_theirs, first_theirs, both_theirs]
        last = [(middle, False), (both, True), (first, True), (middle, True)]
        return tuple(finish(plan, leaf_ids, update, predict, last, pieces, values))

    return jax.shard_map(
        shards,
        mesh=mesh,
        in_specs=(P(None, AXES), P(AXES), P(None, AXES)),
        out_specs=(P(None, AXES), P(None, "leaf")),
        check_vma=False,
    )
```

```python
import functools

import jax
import jax.numpy as jnp
from jax import lax
from jax.experimental import pallas as pl
from jax.experimental.pallas import tpu as pltpu
from jax.sharding import PartitionSpec as P

LEAVES = 64
PAIR = 2 * LEAVES
STEP_SIZE = 0.5
RIDGE_TERM = 1.0
VMEM_LIMIT = 24 * 1024 * 1024
AXES = ("dp", "leaf")
IN_VMEM = pl.BlockSpec(memory_space=pltpu.VMEM)
IN_HBM = pl.BlockSpec(memory_space=pltpu.HBM)


def round_up(value, multiple):
    return -(-value // multiple) * multiple


class Plan:
    def __init__(self, mesh, pairs):
        dp, leaf = mesh.shape["dp"], mesh.shape["leaf"]
        self.leaf = leaf
        self.devices = dp * leaf
        chip_bits = (dp - 1).bit_length() - 1
        low = (chip_bits + 1) // 2
        x_bits = [leaf << (1 + b) for b in range(low)]
        y_bits = [leaf << (1 + b) for b in range(low, chip_bits)]
        z_bits = [1 << b for b in range((leaf - 1).bit_length())]
        even, odd = [], []
        for b in range(low):
            step = [x_bits[b]] + y_bits[b : b + 1]
            even += step
            odd += step[::-1]
        self.core = leaf
        self.masks = [[leaf] + even + z_bits, [leaf] + odd + z_bits[::-1]]
        self.steps = len(self.masks[0])
        self.halvings = 0
        while self.halvings < self.steps and pairs >> (self.halvings + 1) << (self.halvings + 1) == pairs:
            self.halvings += 1
        self.pairs = pairs

    def permutation(self, *steps):
        pairs = []
        for device in range(self.devices):
            partner = device
            for step in steps:
                partner ^= self.masks[1 if device & self.core else 0][step]
            pairs.append((device, partner))
        return pairs

    def code(self, device, other):
        odd = (device & self.core) != 0
        codes = []
        for masks in self.masks:
            total = jnp.int32(0)
            for step in range(1, self.halvings):
                half = self.pairs >> (step + 1)
                total = total | jnp.where((device & masks[step]) != 0, half, 0)
            codes.append(total)
        top = self.pairs >> 1
        if other:
            return jnp.where(odd, codes[0], codes[1] | top)
        return jnp.where(odd, codes[1] | top, codes[0])


def own_device(plan):
    return lax.axis_index("dp").astype(jnp.int32) * plan.leaf + lax.axis_index("leaf").astype(jnp.int32)


def one_hot(ids_ref, rows, first, width):
    slot = lax.broadcasted_iota(jnp.int32, (LEAVES, width), 0).astype(jnp.float32).astype(jnp.bfloat16)
    one, zero = jnp.bfloat16(1), jnp.bfloat16(0)
    blocks = []
    for row in rows:
        ids = ids_ref[pl.ds(row, 1), pl.ds(first, width)].astype(jnp.float32).astype(jnp.bfloat16)
        blocks.append(jnp.where(ids == slot, one, zero))
    return jnp.concatenate(blocks, axis=0)


def tree_rows(code, slots):
    rows = []
    for slot in slots:
        first = (slot ^ code) * 2
        rows += [first, first + 1]
    return rows


def groups(slots, size):
    return [slots[i : i + size] for i in range(0, len(slots), size)]


def chunk(rows, limit):
    width = rows
    while width > limit and width % 256 == 0:
        width //= 2
    return width


def pair_sums(hot, stacked):
    return lax.dot_general(hot, stacked, (((1,), (1,)), ((), ())), preferred_element_type=jnp.float32)


def write_sums(sums, half, out_ref, first):
    classes = out_ref.shape[0]
    turned = sums.T
    for i in range(turned.shape[1] // PAIR):
        block = turned[:, i * PAIR : (i + 1) * PAIR]
        out_ref[:, pl.ds(2 * (first + i) * PAIR, PAIR)] = block[:classes]
        out_ref[:, pl.ds((2 * (first + i) + 1) * PAIR, PAIR)] = block[half : half + classes]


def add_up(plan, parts, half, width, stacked_ref, ids_ref, out_refs):
    device = own_device(plan)
    rows = stacked_ref.shape[1]
    todo = []
    for (slots, other), out_ref in zip(parts, out_refs):
        tree = tree_rows(plan.code(device, other), slots)
        todo += [(tree[2 * i : 2 * i + 2], out_ref, i) for i in range(len(slots))]
    for group in groups(todo, 4):
        tree = [row for item in group for row in item[0]]
        total = None
        for first in range(0, rows, width):
            part = pair_sums(one_hot(ids_ref, tree, first, width), stacked_ref[:, first : first + width])
            total = part if total is None else total + part
        for i, (_, out_ref, place) in enumerate(group):
            write_sums(total[i * PAIR : (i + 1) * PAIR], half, out_ref, place)


def first_kernel(plan, slots, half, width, predict_hbm, labels_hbm, ids_hbm, stacked_ref, other_ref,
                 predict_ref, labels_ref, ids_ref, sems):
    rows = predict_ref.shape[1]
    classes = predict_ref.shape[0]
    count = rows // width
    copies = [
        pltpu.make_async_copy(labels_hbm, labels_ref, sems.at[0]),
        pltpu.make_async_copy(ids_hbm, ids_ref, sems.at[1]),
    ]
    for i in range(count):
        part = pl.ds(i * width, width)
        copies.append(pltpu.make_async_copy(predict_hbm.at[:, part], predict_ref.at[:, part], sems.at[2 + i]))
    copies[2].start()
    copies[0].start()
    for copy in copies[3:]:
        copy.start()
    copies[1].start()
    copies[0].wait()
    for i in range(count):
        copies[2 + i].wait()
        predict = predict_ref[:, i * width : (i + 1) * width]
        row_max = jnp.max(predict, axis=0, keepdims=True)
        exponent = jnp.exp(predict - row_max)
        probability = exponent * (1.0 / jnp.sum(exponent, axis=0, keepdims=True))
        index = lax.broadcasted_iota(jnp.int32, predict.shape, 0)
        gradient = jnp.where(index == labels_ref[:, i * width : (i + 1) * width], probability - 1.0, probability)
        filler = jnp.zeros((half - classes, width), jnp.float32)
        stacked_ref[:, i * width : (i + 1) * width] = jnp.concatenate(
            [gradient, filler, probability * (1.0 - probability), filler], axis=0
        ).astype(jnp.bfloat16)
    copies[1].wait()
    add_up(plan, [(slots, True)], half, width, stacked_ref, ids_ref, (other_ref,))


def sums_kernel(plan, parts, half, width, stacked_ref, ids_ref, _, *out_refs):
    add_up(plan, parts, half, width, stacked_ref, ids_ref, out_refs)


def sums_cost(count, half, rows):
    return pl.CostEstimate(
        flops=2 * count * PAIR * rows * 2 * half, bytes_accessed=2 * half * rows * 2, transcendentals=0
    )


def first_sums(plan, predict, labels, leaf_ids, slots, half):
    classes, rows = predict.shape
    width = chunk(rows, 1024)
    return pl.pallas_call(
        functools.partial(first_kernel, plan, slots, half, width),
        in_specs=[IN_HBM, IN_HBM, IN_HBM],
        out_specs=[IN_VMEM, IN_VMEM],
        out_shape=[
            pltpu.VMEM((2 * half, rows), jnp.bfloat16),
            pltpu.VMEM((classes, 2 * PAIR * len(slots)), jnp.float32),
        ],
        scratch_shapes=[
            pltpu.VMEM((classes, rows), jnp.float32),
            pltpu.VMEM((1, rows), jnp.int32),
            pltpu.VMEM(leaf_ids.shape, jnp.int32),
            pltpu.SemaphoreType.DMA((2 + rows // width,)),
        ],
        compiler_params=pltpu.CompilerParams(vmem_limit_bytes=VMEM_LIMIT),
        cost_estimate=sums_cost(len(slots), half, rows),
        name="gradients_and_sums",
    )(*(pltpu.with_memory_space_constraint(x, pltpu.HBM) for x in (predict, labels.reshape(1, rows), leaf_ids)))


def more_sums(plan, stacked, leaf_ids, classes, parts, earlier):
    height, rows = stacked.shape
    return pl.pallas_call(
        functools.partial(sums_kernel, plan, parts, height // 2, chunk(rows, 1024)),
        in_specs=[IN_VMEM, IN_VMEM, pl.BlockSpec(memory_space=pl.ANY)],
        out_specs=[IN_VMEM] * len(parts),
        out_shape=[jax.ShapeDtypeStruct((classes, 2 * PAIR * len(slots)), jnp.float32) for slots, _ in parts],
        compiler_params=pltpu.CompilerParams(vmem_limit_bytes=VMEM_LIMIT),
        cost_estimate=sums_cost(sum(len(slots) for slots, _ in parts), height // 2, rows),
        name="leaf_sums",
    )(stacked, leaf_ids, earlier)


def looked_up(plan, parts, value_refs, ids_ref, first, width):
    device = own_device(plan)
    todo = []
    for (slots, other), value_ref in zip(parts, value_refs):
        tree = tree_rows(plan.code(device, other), slots)
        todo += [(tree[2 * i : 2 * i + 2], value_ref, i) for i in range(len(slots))]
    total = None
    for group in groups(todo, 2):
        tree = [row for item in group for row in item[0]]
        hot = one_hot(ids_ref, tree, first, width)
        values = [ref[:, pl.ds(i * PAIR, PAIR)].astype(jnp.bfloat16) for _, ref, i in group]
        values = values[0] if len(values) == 1 else jnp.concatenate(values, axis=1)
        part = jnp.dot(values, hot, preferred_element_type=jnp.float32)
        total = part if total is None else total + part
    return total


def apply_kernel(plan, parts, width, carried, *refs):
    ids_ref, refs = refs[0], refs[1:]
    value_refs, out_ref = refs[: len(parts)], refs[-1]
    for first in range(0, out_ref.shape[1], width):
        part = pl.ds(first, width)
        total = looked_up(plan, parts, value_refs, ids_ref, first, width)
        out_ref[:, part] = refs[len(parts)][:, part] + total if carried else total


def apply_cost(count, classes, rows):
    return pl.CostEstimate(
        flops=2 * count * PAIR * rows * 2 * classes, bytes_accessed=4 * classes * rows, transcendentals=0
    )


def apply_values(plan, leaf_ids, parts, values, update):
    classes, rows = values[0].shape[0], leaf_ids.shape[1]
    carried = update is not None
    operands = (leaf_ids, *values) + ((update,) if carried else ())
    return pl.pallas_call(
        functools.partial(apply_kernel, plan, parts, chunk(rows, 2048), carried),
        in_specs=[IN_VMEM] * len(operands),
        out_specs=IN_VMEM,
        out_shape=jax.ShapeDtypeStruct((classes, rows), jnp.float32),
        input_output_aliases={len(operands) - 1: 0} if carried else {},
        compiler_params=pltpu.CompilerParams(vmem_limit_bytes=VMEM_LIMIT),
        cost_estimate=apply_cost(sum(len(slots) for slots, _ in parts), classes, rows),
        name="apply_values",
    )(*operands)


def last_kernel(plan, parts, pieces, width, *refs):
    ids_ref, update_ref, predict_ref = refs[:3]
    value_refs = refs[3 : 3 + len(pieces)]
    out_hbm, own_hbm, out_ref, own_ref, table_ref, sems = refs[3 + len(pieces) :]
    rows = ids_ref.shape[1]
    count = rows // width
    device = own_device(plan)
    half = plan.pairs // 2
    for (slots, other), value_ref in zip(pieces, value_refs):
        first = slots[0] + (half if other else 0)
        table_ref[:, pl.ds(first * PAIR, len(slots) * PAIR)] = value_ref[...]
    mine, theirs = plan.code(device, False), plan.code(device, True)
    per_leaf = plan.pairs // plan.leaf
    for i in range(per_leaf):
        pair = lax.axis_index("leaf").astype(jnp.int32) * per_leaf + i
        place = pair ^ mine
        place = jnp.where(place < half, place, (pair ^ theirs) + half)
        own_ref[:, pl.ds(i * PAIR, PAIR)] = table_ref[:, pl.ds(pl.multiple_of(place * PAIR, PAIR), PAIR)]
    writes = [pltpu.make_async_copy(own_ref, own_hbm, sems.at[count])]
    writes[0].start()
    last = [value_refs[pieces.index(piece)] for piece in parts]
    for i in range(count):
        part = pl.ds(i * width, width)
        total = looked_up(plan, parts, last, ids_ref, i * width, width) + update_ref[:, part]
        out_ref[:, part] = predict_ref[:, part] + total
        writes.append(pltpu.make_async_copy(out_ref.at[:, part], out_hbm.at[:, part], sems.at[i]))
        writes[-1].start()
    for write in writes:
        write.wait()


def finish(plan, leaf_ids, update, predict, parts, pieces, values):
    classes, rows = predict.shape
    width = chunk(rows, 2048)
    own = (classes, plan.pairs // plan.leaf * PAIR)
    return pl.pallas_call(
        functools.partial(last_kernel, plan, parts, pieces, width),
        in_specs=[IN_VMEM] * (3 + len(values)),
        out_specs=[IN_HBM, IN_HBM],
        out_shape=[jax.ShapeDtypeStruct((classes, rows), jnp.float32), jax.ShapeDtypeStruct(own, jnp.float32)],
        scratch_shapes=[
            pltpu.VMEM((classes, rows), jnp.float32),
            pltpu.VMEM(own, jnp.float32),
            pltpu.VMEM((classes, plan.pairs * PAIR), jnp.float32),
            pltpu.SemaphoreType.DMA((rows // width + 1,)),
        ],
        compiler_params=pltpu.CompilerParams(vmem_limit_bytes=VMEM_LIMIT),
        cost_estimate=apply_cost(sum(len(slots) for slots, _ in parts), classes, rows),
        name="apply_last_values",
    )(leaf_ids, update, predict, *values)


def newton(sums):
    values = []
    for i in range(sums.shape[1] // (2 * PAIR)):
        gradient = sums[:, 2 * i * PAIR : (2 * i + 1) * PAIR]
        hessian = sums[:, (2 * i + 1) * PAIR : (2 * i + 2) * PAIR]
        values.append(-STEP_SIZE * gradient / (hessian + RIDGE_TERM))
    return values[0] if len(values) == 1 else jnp.concatenate(values, axis=1)


def solution(mesh):
    def shards(predict, labels, leaf_ids):
        classes = predict.shape[0]
        plan = Plan(mesh, leaf_ids.shape[0] // 2)
        half = round_up(classes, 16)

        def exchange(value, *steps):
            return lax.ppermute(value, AXES, plan.permutation(*steps))

        h = plan.pairs // 2
        unit = h // 8
        far = list(range(h // 2, h))
        near = list(range(h // 2))
        own, by_3, by_2, by_both = (near[i * unit : (i + 1) * unit] for i in range(4))

        stacked, far_other = first_sums(plan, predict, labels, leaf_ids, far, half)
        (far_own,) = more_sums(plan, stacked, leaf_ids, classes, [(far, False)], far_other)
        far_sums = far_own + exchange(far_other, 0)
        far_moved = exchange(far_sums, 1)
        near_other, upper_own = more_sums(
            plan, stacked, leaf_ids, classes, [(near, True), (by_2 + by_both, False)], far_sums
        )
        near_core = exchange(near_other, 0)
        (lower_own,) = more_sums(plan, stacked, leaf_ids, classes, [(own + by_3, False)], near_other)

        def quarter(i):
            part = slice(2 * PAIR * unit * i, 2 * PAIR * unit * (i + 1))
            inner = slice(2 * PAIR * unit * (i % 2), 2 * PAIR * unit * (i % 2 + 1))
            return (upper_own if i > 1 else lower_own)[:, inner] + near_core[:, part] + far_moved[:, part]

        held = quarter(0)
        held = held + exchange(quarter(3), 2, 3) + exchange(quarter(1), 3) + exchange(quarter(2), 2)
        for step in range(4, plan.steps):
            if step < plan.halvings:
                keep = held.shape[1] // 2
                held = held[:, :keep] + exchange(held[:, keep:], step)
            else:
                held = held + exchange(held, step)
        values = newton(held)
        for step in reversed(range(4, plan.halvings)):
            values = jnp.concatenate([values, exchange(values, step)], axis=1)

        moved = [exchange(values, 3), exchange(values, 2), exchange(values, 2, 3)]
        near_values = jnp.concatenate([values] + moved, axis=1)
        far_values = exchange(near_values, 1)
        near_theirs = exchange(near_values, 0)
        update = apply_values(
            plan, leaf_ids, [(near, False), (near, True)], [near_values, near_theirs], None
        )
        far_values, update = lax.optimization_barrier((far_values, update))
        far_theirs = exchange(far_values, 0)
        update = apply_values(plan, leaf_ids, [(far, False)], [far_values], update)
        pieces = [(near, False), (far, False), (near, True), (far, True)]
        values = [near_values, far_values, near_theirs, far_theirs]
        return tuple(finish(plan, leaf_ids, update, predict, [(far, True)], pieces, values))

    return jax.shard_map(
        shards,
        mesh=mesh,
        in_specs=(P(None, AXES), P(AXES), P(None, AXES)),
        out_specs=(P(None, AXES), P(None, "leaf")),
        check_vma=False,
    )
```

```python
import functools

import jax
import jax.numpy as jnp
from jax import lax
from jax.experimental import pallas as pl
from jax.experimental.pallas import tpu as pltpu
from jax.sharding import PartitionSpec as P

LEAVES = 64
PAIR = 2 * LEAVES
STEP_SIZE = 0.5
RIDGE_TERM = 1.0
VMEM_LIMIT = 24 * 1024 * 1024
AXES = ("dp", "leaf")
IN_VMEM = pl.BlockSpec(memory_space=pltpu.VMEM)
IN_HBM = pl.BlockSpec(memory_space=pltpu.HBM)


def round_up(value, multiple):
    return -(-value // multiple) * multiple


class Plan:
    def __init__(self, mesh, pairs):
        dp, leaf = mesh.shape["dp"], mesh.shape["leaf"]
        self.leaf = leaf
        self.devices = dp * leaf
        chip_bits = (dp - 1).bit_length() - 1
        low = (chip_bits + 1) // 2
        x_bits = [leaf << (1 + b) for b in range(low)]
        y_bits = [leaf << (1 + b) for b in range(low, chip_bits)]
        z_bits = [1 << b for b in range((leaf - 1).bit_length())]
        even, odd = [], []
        for b in range(low):
            step = [x_bits[b]] + y_bits[b : b + 1]
            even += step
            odd += step[::-1]
        self.core = leaf
        self.masks = [[leaf] + even + z_bits, [leaf] + odd + z_bits]
        self.steps = len(self.masks[0])
        self.halvings = 0
        while self.halvings < self.steps and pairs >> (self.halvings + 1) << (self.halvings + 1) == pairs:
            self.halvings += 1
        self.pairs = pairs

    def permutation(self, *steps):
        pairs = []
        for device in range(self.devices):
            partner = device
            for step in steps:
                partner ^= self.masks[1 if device & self.core else 0][step]
            pairs.append((device, partner))
        return pairs

    def code(self, device, other):
        odd = (device & self.core) != 0
        codes = []
        for masks in self.masks:
            total = jnp.int32(0)
            for step in range(1, self.halvings):
                half = self.pairs >> (step + 1)
                total = total | jnp.where((device & masks[step]) != 0, half, 0)
            codes.append(total)
        top = self.pairs >> 1
        if other:
            return jnp.where(odd, codes[0], codes[1] | top)
        return jnp.where(odd, codes[1] | top, codes[0])


def own_device(plan):
    return lax.axis_index("dp").astype(jnp.int32) * plan.leaf + lax.axis_index("leaf").astype(jnp.int32)


def one_hot(ids_ref, rows, first, width):
    slot = lax.broadcasted_iota(jnp.int32, (LEAVES, width), 0).astype(jnp.float32).astype(jnp.bfloat16)
    one, zero = jnp.bfloat16(1), jnp.bfloat16(0)
    blocks = []
    for row in rows:
        ids = ids_ref[pl.ds(row, 1), pl.ds(first, width)].astype(jnp.float32).astype(jnp.bfloat16)
        blocks.append(jnp.where(ids == slot, one, zero))
    return jnp.concatenate(blocks, axis=0)


def tree_rows(code, slots):
    rows = []
    for slot in slots:
        first = (slot ^ code) * 2
        rows += [first, first + 1]
    return rows


def groups(slots, size):
    return [slots[i : i + size] for i in range(0, len(slots), size)]


def chunk(rows, limit):
    width = rows
    while width > limit and width % 256 == 0:
        width //= 2
    return width


def pair_sums(hot, stacked):
    return lax.dot_general(hot, stacked, (((1,), (1,)), ((), ())), preferred_element_type=jnp.float32)


def write_sums(sums, half, out_ref, first):
    classes = out_ref.shape[0]
    turned = sums.T
    for i in range(turned.shape[1] // PAIR):
        block = turned[:, i * PAIR : (i + 1) * PAIR]
        out_ref[:, pl.ds(2 * (first + i) * PAIR, PAIR)] = block[:classes]
        out_ref[:, pl.ds((2 * (first + i) + 1) * PAIR, PAIR)] = block[half : half + classes]


def add_up(plan, parts, half, width, stacked_ref, ids_ref, out_refs, start=0):
    device = own_device(plan)
    rows = stacked_ref.shape[1]
    todo = []
    for (slots, other), out_ref in zip(parts, out_refs):
        tree = tree_rows(plan.code(device, other), slots)
        todo += [(tree[2 * i : 2 * i + 2], out_ref, i) for i in range(len(slots))]
    for group in groups(todo, 4):
        tree = [row - start for item in group for row in item[0]]
        total = None
        for first in range(0, rows, width):
            part = pair_sums(one_hot(ids_ref, tree, first, width), stacked_ref[:, first : first + width])
            total = part if total is None else total + part
        for i, (_, out_ref, place) in enumerate(group):
            write_sums(total[i * PAIR : (i + 1) * PAIR], half, out_ref, place)


def first_kernel(plan, slots, half, width, predict_hbm, labels_hbm, ids_hbm, stacked_ref, other_ref,
                 predict_ref, labels_ref, ids_ref, sems):
    rows = predict_ref.shape[1]
    classes = predict_ref.shape[0]
    count = rows // width
    group = pl.multiple_of(tree_rows(plan.code(own_device(plan), True), [slots[0]])[0] & -len(slots) * 2, 8)
    copies = [
        pltpu.make_async_copy(labels_hbm, labels_ref, sems.at[0]),
        pltpu.make_async_copy(ids_hbm.at[pl.ds(group, ids_ref.shape[0]), :], ids_ref, sems.at[1]),
    ]
    for i in range(count):
        part = pl.ds(i * width, width)
        copies.append(pltpu.make_async_copy(predict_hbm.at[:, part], predict_ref.at[:, part], sems.at[2 + i]))
    copies[2].start()
    copies[0].start()
    for copy in copies[3:]:
        copy.start()
    copies[1].start()
    copies[0].wait()
    for i in range(count):
        copies[2 + i].wait()
        predict = predict_ref[:, i * width : (i + 1) * width]
        row_max = jnp.max(predict, axis=0, keepdims=True)
        exponent = jnp.exp(predict - row_max)
        probability = exponent * (1.0 / jnp.sum(exponent, axis=0, keepdims=True))
        index = lax.broadcasted_iota(jnp.int32, predict.shape, 0)
        gradient = jnp.where(index == labels_ref[:, i * width : (i + 1) * width], probability - 1.0, probability)
        filler = jnp.zeros((half - classes, width), jnp.float32)
        stacked_ref[:, i * width : (i + 1) * width] = jnp.concatenate(
            [gradient, filler, probability * (1.0 - probability), filler], axis=0
        ).astype(jnp.bfloat16)
    copies[1].wait()
    add_up(plan, [(slots, True)], half, width, stacked_ref, ids_ref, (other_ref,), group)


def sums_kernel(plan, parts, half, width, stacked_ref, ids_ref, _, *out_refs):
    add_up(plan, parts, half, width, stacked_ref, ids_ref, out_refs)


def sums_cost(count, half, rows):
    return pl.CostEstimate(
        flops=2 * count * PAIR * rows * 2 * half, bytes_accessed=2 * half * rows * 2, transcendentals=0
    )


def first_sums(plan, predict, labels, leaf_ids, slots, half):
    classes, rows = predict.shape
    width = chunk(rows, 1024)
    return pl.pallas_call(
        functools.partial(first_kernel, plan, slots, half, width),
        in_specs=[IN_HBM, IN_HBM, IN_HBM],
        out_specs=[IN_VMEM, IN_VMEM],
        out_shape=[
            pltpu.VMEM((2 * half, rows), jnp.bfloat16),
            pltpu.VMEM((classes, 2 * PAIR * len(slots)), jnp.float32),
        ],
        scratch_shapes=[
            pltpu.VMEM((classes, rows), jnp.float32),
            pltpu.VMEM((1, rows), jnp.int32),
            pltpu.VMEM((2 * len(slots), rows), jnp.int32),
            pltpu.SemaphoreType.DMA((2 + rows // width,)),
        ],
        compiler_params=pltpu.CompilerParams(vmem_limit_bytes=VMEM_LIMIT),
        cost_estimate=sums_cost(len(slots), half, rows),
        name="gradients_and_sums",
    )(*(pltpu.with_memory_space_constraint(x, pltpu.HBM) for x in (predict, labels.reshape(1, rows), leaf_ids)))


def more_sums(plan, stacked, leaf_ids, classes, parts, earlier):
    height, rows = stacked.shape
    return pl.pallas_call(
        functools.partial(sums_kernel, plan, parts, height // 2, chunk(rows, 2048)),
        in_specs=[IN_VMEM, IN_VMEM, pl.BlockSpec(memory_space=pl.ANY)],
        out_specs=[IN_VMEM] * len(parts),
        out_shape=[jax.ShapeDtypeStruct((classes, 2 * PAIR * len(slots)), jnp.float32) for slots, _ in parts],
        compiler_params=pltpu.CompilerParams(vmem_limit_bytes=VMEM_LIMIT),
        cost_estimate=sums_cost(sum(len(slots) for slots, _ in parts), height // 2, rows),
        name="leaf_sums",
    )(stacked, leaf_ids, earlier)


def looked_up(plan, parts, value_refs, ids_ref, first, width):
    device = own_device(plan)
    todo = []
    for (slots, other), value_ref in zip(parts, value_refs):
        tree = tree_rows(plan.code(device, other), slots)
        todo += [(tree[2 * i : 2 * i + 2], value_ref, i) for i in range(len(slots))]
    total = None
    for group in groups(todo, 2):
        tree = [row for item in group for row in item[0]]
        hot = one_hot(ids_ref, tree, first, width)
        values = [ref[:, pl.ds(i * PAIR, PAIR)].astype(jnp.bfloat16) for _, ref, i in group]
        values = values[0] if len(values) == 1 else jnp.concatenate(values, axis=1)
        part = jnp.dot(values, hot, preferred_element_type=jnp.float32)
        total = part if total is None else total + part
    return total


def apply_kernel(plan, parts, width, ids_ref, carried_ref, *refs):
    value_refs, out_ref = refs[:-1], refs[-1]
    for first in range(0, out_ref.shape[1], width):
        part = pl.ds(first, width)
        out_ref[:, part] = carried_ref[:, part] + looked_up(plan, parts, value_refs, ids_ref, first, width)


def apply_cost(count, classes, rows):
    return pl.CostEstimate(
        flops=2 * count * PAIR * rows * 2 * classes, bytes_accessed=4 * classes * rows, transcendentals=0
    )


def apply_values(plan, leaf_ids, parts, values, carried):
    classes, rows = carried.shape
    return pl.pallas_call(
        functools.partial(apply_kernel, plan, parts, chunk(rows, 2048)),
        in_specs=[IN_VMEM] * (2 + len(values)),
        out_specs=IN_VMEM,
        out_shape=jax.ShapeDtypeStruct((classes, rows), jnp.float32),
        compiler_params=pltpu.CompilerParams(vmem_limit_bytes=VMEM_LIMIT),
        cost_estimate=apply_cost(sum(len(slots) for slots, _ in parts), classes, rows),
        name="apply_values",
    )(leaf_ids, carried, *values)


def last_kernel(plan, parts, pieces, width, *refs):
    ids_ref, carried_ref = refs[:2]
    value_refs = refs[2 : 2 + len(pieces)]
    out_hbm, own_hbm, out_ref, own_ref, table_ref, sems = refs[2 + len(pieces) :]
    rows = ids_ref.shape[1]
    count = rows // width
    device = own_device(plan)
    half = plan.pairs // 2
    for (slots, other), value_ref in zip(pieces, value_refs):
        first = slots[0] + (half if other else 0)
        table_ref[:, pl.ds(first * PAIR, len(slots) * PAIR)] = value_ref[...]
    mine, theirs = plan.code(device, False), plan.code(device, True)
    per_leaf = plan.pairs // plan.leaf
    for i in range(per_leaf):
        pair = lax.axis_index("leaf").astype(jnp.int32) * per_leaf + i
        place = pair ^ mine
        place = jnp.where(place < half, place, (pair ^ theirs) + half)
        own_ref[:, pl.ds(i * PAIR, PAIR)] = table_ref[:, pl.ds(pl.multiple_of(place * PAIR, PAIR), PAIR)]
    writes = []
    last = [value_refs[pieces.index(piece)] for piece in parts]
    for i in range(count):
        part = pl.ds(i * width, width)
        out_ref[:, part] = carried_ref[:, part] + looked_up(plan, parts, last, ids_ref, i * width, width)
        writes.append(pltpu.make_async_copy(out_ref.at[:, part], out_hbm.at[:, part], sems.at[i]))
        writes[-1].start()
        if i == 0:
            writes.append(pltpu.make_async_copy(own_ref, own_hbm, sems.at[count]))
            writes[-1].start()
    for write in writes:
        write.wait()


def finish(plan, leaf_ids, carried, parts, pieces, values):
    classes, rows = carried.shape
    width = chunk(rows, 1024)
    own = (classes, plan.pairs // plan.leaf * PAIR)
    return pl.pallas_call(
        functools.partial(last_kernel, plan, parts, pieces, width),
        in_specs=[IN_VMEM] * (2 + len(values)),
        out_specs=[IN_HBM, IN_HBM],
        out_shape=[jax.ShapeDtypeStruct((classes, rows), jnp.float32), jax.ShapeDtypeStruct(own, jnp.float32)],
        scratch_shapes=[
            pltpu.VMEM((classes, rows), jnp.float32),
            pltpu.VMEM(own, jnp.float32),
            pltpu.VMEM((classes, plan.pairs * PAIR), jnp.float32),
            pltpu.SemaphoreType.DMA((rows // width + 1,)),
        ],
        compiler_params=pltpu.CompilerParams(vmem_limit_bytes=VMEM_LIMIT),
        cost_estimate=apply_cost(sum(len(slots) for slots, _ in parts), classes, rows),
        name="apply_last_values",
    )(leaf_ids, carried, *values)


def newton(sums):
    values = []
    for i in range(sums.shape[1] // (2 * PAIR)):
        gradient = sums[:, 2 * i * PAIR : (2 * i + 1) * PAIR]
        hessian = sums[:, (2 * i + 1) * PAIR : (2 * i + 2) * PAIR]
        values.append(-STEP_SIZE * gradient / (hessian + RIDGE_TERM))
    return values[0] if len(values) == 1 else jnp.concatenate(values, axis=1)


def solution(mesh):
    def shards(predict, labels, leaf_ids):
        classes = predict.shape[0]
        plan = Plan(mesh, leaf_ids.shape[0] // 2)
        half = round_up(classes, 16)

        def exchange(value, *steps):
            return lax.ppermute(value, AXES, plan.permutation(*steps))

        h = plan.pairs // 2
        unit = h // 8
        far = list(range(h // 2, h))
        near = list(range(h // 2))
        own, by_3, by_2, by_both = (near[i * unit : (i + 1) * unit] for i in range(4))

        stacked, far_other = first_sums(plan, predict, labels, leaf_ids, far, half)
        (far_own,) = more_sums(plan, stacked, leaf_ids, classes, [(far, False)], far_other)
        far_sums = far_own + exchange(far_other, 0)
        far_moved = exchange(far_sums, 1)
        near_other, upper_own = more_sums(
            plan, stacked, leaf_ids, classes, [(near, True), (by_2 + by_both, False)], far_sums
        )
        near_core = exchange(near_other, 0)
        (lower_own,) = more_sums(plan, stacked, leaf_ids, classes, [(own + by_3, False)], near_other)

        def quarter(i):
            part = slice(2 * PAIR * unit * i, 2 * PAIR * unit * (i + 1))
            inner = slice(2 * PAIR * unit * (i % 2), 2 * PAIR * unit * (i % 2 + 1))
            return (upper_own if i > 1 else lower_own)[:, inner] + near_core[:, part] + far_moved[:, part]

        held = quarter(0)
        held = held + exchange(quarter(3), 2, 3) + exchange(quarter(1), 3) + exchange(quarter(2), 2)
        for step in range(4, plan.steps):
            if step < plan.halvings:
                keep = held.shape[1] // 2
                held = held[:, :keep] + exchange(held[:, keep:], step)
            else:
                held = held + exchange(held, step)
        values = newton(held)
        for step in reversed(range(4, plan.halvings)):
            values = jnp.concatenate([values, exchange(values, step)], axis=1)

        moved = [exchange(values, 3), exchange(values, 2), exchange(values, 2, 3)]
        near_values = jnp.concatenate([values] + moved, axis=1)
        far_values = exchange(near_values, 1)
        near_theirs = exchange(near_values, 0)
        update = apply_values(
            plan, leaf_ids, [(near, False), (near, True)], [near_values, near_theirs], predict
        )
        far_values, update = lax.optimization_barrier((far_values, update))
        far_theirs = exchange(far_values, 0)
        update = apply_values(plan, leaf_ids, [(far, False)], [far_values], update)
        pieces = [(near, False), (far, False), (near, True), (far, True)]
        values = [near_values, far_values, near_theirs, far_theirs]
        return tuple(finish(plan, leaf_ids, update, [(far, True)], pieces, values))

    return jax.shard_map(
        shards,
        mesh=mesh,
        in_specs=(P(None, AXES), P(AXES), P(None, AXES)),
        out_specs=(P(None, AXES), P(None, "leaf")),
        check_vma=False,
    )
```

```python
import functools

import jax
import jax.numpy as jnp
from jax import lax
from jax.experimental import pallas as pl
from jax.experimental.pallas import tpu as pltpu
from jax.sharding import PartitionSpec as P

LEAVES = 64
PAIR = 2 * LEAVES
STEP_SIZE = 0.5
RIDGE_TERM = 1.0
VMEM_LIMIT = 24 * 1024 * 1024
AXES = ("dp", "leaf")
IN_VMEM = pl.BlockSpec(memory_space=pltpu.VMEM)
IN_HBM = pl.BlockSpec(memory_space=pltpu.HBM)


def round_up(value, multiple):
    return -(-value // multiple) * multiple


class Plan:
    def __init__(self, mesh, pairs):
        dp, leaf = mesh.shape["dp"], mesh.shape["leaf"]
        self.leaf = leaf
        self.devices = dp * leaf
        chip_bits = (dp - 1).bit_length() - 1
        low = (chip_bits + 1) // 2
        x_bits = [leaf << (1 + b) for b in range(low)]
        y_bits = [leaf << (1 + b) for b in range(low, chip_bits)]
        z_bits = [1 << b for b in range((leaf - 1).bit_length())]
        even, odd = [], []
        for b in range(low):
            step = [x_bits[b]] + y_bits[b : b + 1]
            even += step
            odd += step[::-1]
        self.core = leaf
        self.masks = [[leaf] + even + z_bits, [leaf] + odd + z_bits]
        self.steps = len(self.masks[0])
        self.halvings = 0
        while self.halvings < self.steps and pairs >> (self.halvings + 1) << (self.halvings + 1) == pairs:
            self.halvings += 1
        self.pairs = pairs

    def permutation(self, *steps):
        pairs = []
        for device in range(self.devices):
            partner = device
            for step in steps:
                partner ^= self.masks[1 if device & self.core else 0][step]
            pairs.append((device, partner))
        return pairs

    def code(self, device, other):
        odd = (device & self.core) != 0
        codes = []
        for masks in self.masks:
            total = jnp.int32(0)
            for step in range(1, self.halvings):
                half = self.pairs >> (step + 1)
                total = total | jnp.where((device & masks[step]) != 0, half, 0)
            codes.append(total)
        top = self.pairs >> 1
        if other:
            return jnp.where(odd, codes[0], codes[1] | top)
        return jnp.where(odd, codes[1] | top, codes[0])


def own_device(plan):
    return lax.axis_index("dp").astype(jnp.int32) * plan.leaf + lax.axis_index("leaf").astype(jnp.int32)


def one_hot(ids_ref, rows, first, width):
    slot = lax.broadcasted_iota(jnp.int32, (LEAVES, width), 0).astype(jnp.float32).astype(jnp.bfloat16)
    one, zero = jnp.bfloat16(1), jnp.bfloat16(0)
    blocks = []
    for row in rows:
        ids = ids_ref[pl.ds(row, 1), pl.ds(first, width)].astype(jnp.float32).astype(jnp.bfloat16)
        blocks.append(jnp.where(ids == slot, one, zero))
    return jnp.concatenate(blocks, axis=0)


def tree_rows(code, slots):
    rows = []
    for slot in slots:
        first = (slot ^ code) * 2
        rows += [first, first + 1]
    return rows


def groups(slots, size):
    return [slots[i : i + size] for i in range(0, len(slots), size)]


def chunk(rows, limit):
    width = rows
    while width > limit and width % 256 == 0:
        width //= 2
    return width


def pair_sums(hot, stacked):
    return lax.dot_general(hot, stacked, (((1,), (1,)), ((), ())), preferred_element_type=jnp.float32)


def write_sums(sums, out_ref, first):
    turned = sums.T[: out_ref.shape[0]]
    out_ref[:, pl.ds(first * PAIR, turned.shape[1])] = turned


def add_up(plan, parts, width, stacked_ref, ids_ref, out_refs, start=0):
    device = own_device(plan)
    rows = stacked_ref.shape[1]
    todo = []
    for (slots, other), out_ref in zip(parts, out_refs):
        tree = tree_rows(plan.code(device, other), slots)
        todo += [(tree[2 * i : 2 * i + 2], out_ref, i) for i in range(len(slots))]
    for group in groups(todo, 4):
        tree = [row - start for item in group for row in item[0]]
        total = None
        for first in range(0, rows, width):
            part = pair_sums(one_hot(ids_ref, tree, first, width), stacked_ref[:, first : first + width])
            total = part if total is None else total + part
        for i, (_, out_ref, place) in enumerate(group):
            write_sums(total[i * PAIR : (i + 1) * PAIR], out_ref, place)


def first_kernel(plan, slots, width, predict_hbm, labels_hbm, ids_hbm, stacked_ref, other_ref,
                 predict_ref, labels_ref, ids_ref, sems):
    rows = predict_ref.shape[1]
    classes = predict_ref.shape[0]
    count = rows // width
    group = pl.multiple_of(tree_rows(plan.code(own_device(plan), True), [slots[0]])[0] & -len(slots) * 2, 8)
    copies = [
        pltpu.make_async_copy(labels_hbm, labels_ref, sems.at[0]),
        pltpu.make_async_copy(ids_hbm.at[pl.ds(group, ids_ref.shape[0]), :], ids_ref, sems.at[1]),
    ]
    for i in range(count):
        part = pl.ds(i * width, width)
        copies.append(pltpu.make_async_copy(predict_hbm.at[:, part], predict_ref.at[:, part], sems.at[2 + i]))
    copies[2].start()
    copies[0].start()
    for copy in copies[3:]:
        copy.start()
    copies[1].start()
    copies[0].wait()
    for i in range(count):
        copies[2 + i].wait()
        predict = predict_ref[:, i * width : (i + 1) * width]
        row_max = jnp.max(predict, axis=0, keepdims=True)
        exponent = jnp.exp(predict - row_max)
        probability = exponent * (1.0 / jnp.sum(exponent, axis=0, keepdims=True))
        index = lax.broadcasted_iota(jnp.int32, predict.shape, 0)
        gradient = jnp.where(index == labels_ref[:, i * width : (i + 1) * width], probability - 1.0, probability)
        filler = jnp.zeros((stacked_ref.shape[0] - 2 * classes, width), jnp.float32)
        stacked_ref[:, i * width : (i + 1) * width] = jnp.concatenate(
            [gradient, probability * (1.0 - probability), filler], axis=0
        ).astype(jnp.bfloat16)
    copies[1].wait()
    add_up(plan, [(slots, True)], width, stacked_ref, ids_ref, (other_ref,), group)


def sums_kernel(plan, parts, width, stacked_ref, ids_ref, _, *out_refs):
    add_up(plan, parts, width, stacked_ref, ids_ref, out_refs)


def sums_cost(count, height, rows):
    return pl.CostEstimate(
        flops=2 * count * PAIR * rows * height, bytes_accessed=2 * height * rows, transcendentals=0
    )


def first_sums(plan, predict, labels, leaf_ids, slots):
    classes, rows = predict.shape
    height = round_up(2 * classes, 16)
    width = chunk(rows, 1024)
    return pl.pallas_call(
        functools.partial(first_kernel, plan, slots, width),
        in_specs=[IN_HBM, IN_HBM, IN_HBM],
        out_specs=[IN_VMEM, IN_VMEM],
        out_shape=[
            pltpu.VMEM((height, rows), jnp.bfloat16),
            pltpu.VMEM((2 * classes, PAIR * len(slots)), jnp.float32),
        ],
        scratch_shapes=[
            pltpu.VMEM((classes, rows), jnp.float32),
            pltpu.VMEM((1, rows), jnp.int32),
            pltpu.VMEM((2 * len(slots), rows), jnp.int32),
            pltpu.SemaphoreType.DMA((2 + rows // width,)),
        ],
        compiler_params=pltpu.CompilerParams(vmem_limit_bytes=VMEM_LIMIT),
        cost_estimate=sums_cost(len(slots), height, rows),
        name="gradients_and_sums",
    )(*(pltpu.with_memory_space_constraint(x, pltpu.HBM) for x in (predict, labels.reshape(1, rows), leaf_ids)))


def more_sums(plan, stacked, leaf_ids, classes, parts, earlier):
    height, rows = stacked.shape
    return pl.pallas_call(
        functools.partial(sums_kernel, plan, parts, chunk(rows, 2048)),
        in_specs=[IN_VMEM, IN_VMEM, pl.BlockSpec(memory_space=pl.ANY)],
        out_specs=[IN_VMEM] * len(parts),
        out_shape=[jax.ShapeDtypeStruct((2 * classes, PAIR * len(slots)), jnp.float32) for slots, _ in parts],
        compiler_params=pltpu.CompilerParams(vmem_limit_bytes=VMEM_LIMIT),
        cost_estimate=sums_cost(sum(len(slots) for slots, _ in parts), height, rows),
        name="leaf_sums",
    )(stacked, leaf_ids, earlier)


def looked_up(plan, parts, value_refs, ids_ref, first, width):
    device = own_device(plan)
    todo = []
    for (slots, other), value_ref in zip(parts, value_refs):
        tree = tree_rows(plan.code(device, other), slots)
        todo += [(tree[2 * i : 2 * i + 2], value_ref, i) for i in range(len(slots))]
    total = None
    for group in groups(todo, 2):
        tree = [row for item in group for row in item[0]]
        hot = one_hot(ids_ref, tree, first, width)
        values = [ref[:, pl.ds(i * PAIR, PAIR)].astype(jnp.bfloat16) for _, ref, i in group]
        values = values[0] if len(values) == 1 else jnp.concatenate(values, axis=1)
        part = jnp.dot(values, hot, preferred_element_type=jnp.float32)
        total = part if total is None else total + part
    return total


def apply_kernel(plan, parts, width, ids_ref, carried_ref, *refs):
    value_refs, out_ref = refs[:-1], refs[-1]
    for first in range(0, out_ref.shape[1], width):
        part = pl.ds(first, width)
        out_ref[:, part] = carried_ref[:, part] + looked_up(plan, parts, value_refs, ids_ref, first, width)


def apply_cost(count, classes, rows):
    return pl.CostEstimate(
        flops=2 * count * PAIR * rows * 2 * classes, bytes_accessed=4 * classes * rows, transcendentals=0
    )


def apply_values(plan, leaf_ids, parts, values, carried):
    classes, rows = carried.shape
    return pl.pallas_call(
        functools.partial(apply_kernel, plan, parts, chunk(rows, 2048)),
        in_specs=[IN_VMEM] * (2 + len(values)),
        out_specs=IN_VMEM,
        out_shape=jax.ShapeDtypeStruct((classes, rows), jnp.float32),
        compiler_params=pltpu.CompilerParams(vmem_limit_bytes=VMEM_LIMIT),
        cost_estimate=apply_cost(sum(len(slots) for slots, _ in parts), classes, rows),
        name="apply_values",
    )(leaf_ids, carried, *values)


def last_kernel(plan, parts, pieces, width, *refs):
    ids_ref, carried_ref = refs[:2]
    value_refs = refs[2 : 2 + len(pieces)]
    out_hbm, own_hbm, out_ref, own_ref, table_ref, sems = refs[2 + len(pieces) :]
    rows = ids_ref.shape[1]
    count = rows // width
    device = own_device(plan)
    half = plan.pairs // 2
    for (slots, other), value_ref in zip(pieces, value_refs):
        first = slots[0] + (half if other else 0)
        table_ref[:, pl.ds(first * PAIR, len(slots) * PAIR)] = value_ref[...]
    mine, theirs = plan.code(device, False), plan.code(device, True)
    per_leaf = plan.pairs // plan.leaf
    for i in range(per_leaf):
        pair = lax.axis_index("leaf").astype(jnp.int32) * per_leaf + i
        place = pair ^ mine
        place = jnp.where(place < half, place, (pair ^ theirs) + half)
        own_ref[:, pl.ds(i * PAIR, PAIR)] = table_ref[:, pl.ds(pl.multiple_of(place * PAIR, PAIR), PAIR)]
    writes = []
    last = [value_refs[pieces.index(piece)] for piece in parts]
    for i in range(count):
        part = pl.ds(i * width, width)
        out_ref[:, part] = carried_ref[:, part] + looked_up(plan, parts, last, ids_ref, i * width, width)
        writes.append(pltpu.make_async_copy(out_ref.at[:, part], out_hbm.at[:, part], sems.at[i]))
        writes[-1].start()
        if i == 0:
            writes.append(pltpu.make_async_copy(own_ref, own_hbm, sems.at[count]))
            writes[-1].start()
    for write in writes:
        write.wait()


def finish(plan, leaf_ids, carried, parts, pieces, values):
    classes, rows = carried.shape
    width = chunk(rows, 1024)
    own = (classes, plan.pairs // plan.leaf * PAIR)
    return pl.pallas_call(
        functools.partial(last_kernel, plan, parts, pieces, width),
        in_specs=[IN_VMEM] * (2 + len(values)),
        out_specs=[IN_HBM, IN_HBM],
        out_shape=[jax.ShapeDtypeStruct((classes, rows), jnp.float32), jax.ShapeDtypeStruct(own, jnp.float32)],
        scratch_shapes=[
            pltpu.VMEM((classes, rows), jnp.float32),
            pltpu.VMEM(own, jnp.float32),
            pltpu.VMEM((classes, plan.pairs * PAIR), jnp.float32),
            pltpu.SemaphoreType.DMA((rows // width + 1,)),
        ],
        compiler_params=pltpu.CompilerParams(vmem_limit_bytes=VMEM_LIMIT),
        cost_estimate=apply_cost(sum(len(slots) for slots, _ in parts), classes, rows),
        name="apply_last_values",
    )(leaf_ids, carried, *values)


def newton(sums):
    classes = sums.shape[0] // 2
    return -STEP_SIZE * sums[:classes] / (sums[classes:] + RIDGE_TERM)


def solution(mesh):
    def shards(predict, labels, leaf_ids):
        classes = predict.shape[0]
        plan = Plan(mesh, leaf_ids.shape[0] // 2)

        def exchange(value, *steps):
            return lax.ppermute(value, AXES, plan.permutation(*steps))

        h = plan.pairs // 2
        unit = h // 8
        far = list(range(h // 2, h))
        near = list(range(h // 2))
        own, by_3, by_2, by_both = (near[i * unit : (i + 1) * unit] for i in range(4))

        stacked, far_other = first_sums(plan, predict, labels, leaf_ids, far)
        (far_own,) = more_sums(plan, stacked, leaf_ids, classes, [(far, False)], far_other)
        far_sums = far_own + exchange(far_other, 0)
        far_moved = exchange(far_sums, 1)
        near_other, upper_own = more_sums(
            plan, stacked, leaf_ids, classes, [(near, True), (by_2 + by_both, False)], far_sums
        )
        near_core = exchange(near_other, 0)
        (lower_own,) = more_sums(plan, stacked, leaf_ids, classes, [(own + by_3, False)], near_other)

        def quarter(i):
            part = slice(PAIR * unit * i, PAIR * unit * (i + 1))
            inner = slice(PAIR * unit * (i % 2), PAIR * unit * (i % 2 + 1))
            return (upper_own if i > 1 else lower_own)[:, inner] + near_core[:, part] + far_moved[:, part]

        held = quarter(0)
        held = held + exchange(quarter(3), 2, 3) + exchange(quarter(1), 3) + exchange(quarter(2), 2)
        for step in range(4, plan.steps):
            if step < plan.halvings:
                keep = held.shape[1] // 2
                held = held[:, :keep] + exchange(held[:, keep:], step)
            else:
                held = held + exchange(held, step)
        values = newton(held)
        for step in reversed(range(4, plan.halvings)):
            values = jnp.concatenate([values, exchange(values, step)], axis=1)

        moved = [exchange(values, 3), exchange(values, 2), exchange(values, 2, 3)]
        near_values = jnp.concatenate([values] + moved, axis=1)
        far_values = exchange(near_values, 1)
        near_theirs = exchange(near_values, 0)
        update = apply_values(
            plan, leaf_ids, [(near, False), (near, True)], [near_values, near_theirs], predict
        )
        far_values, update = lax.optimization_barrier((far_values, update))
        far_theirs = exchange(far_values, 0)
        update = apply_values(plan, leaf_ids, [(far, False)], [far_values], update)
        pieces = [(near, False), (far, False), (near, True), (far, True)]
        values = [near_values, far_values, near_theirs, far_theirs]
        return tuple(finish(plan, leaf_ids, update, [(far, True)], pieces, values))

    return jax.shard_map(
        shards,
        mesh=mesh,
        in_specs=(P(None, AXES), P(AXES), P(None, AXES)),
        out_specs=(P(None, AXES), P(None, "leaf")),
        check_vma=False,
    )
```

```python
import functools

import jax
import jax.numpy as jnp
from jax import lax
from jax.experimental import pallas as pl
from jax.experimental.pallas import tpu as pltpu
from jax.sharding import PartitionSpec as P

LEAVES = 64
PAIR = 2 * LEAVES
STEP_SIZE = 0.5
RIDGE_TERM = 1.0
VMEM_LIMIT = 24 * 1024 * 1024
AXES = ("dp", "leaf")
IN_VMEM = pl.BlockSpec(memory_space=pltpu.VMEM)
IN_HBM = pl.BlockSpec(memory_space=pltpu.HBM)


def round_up(value, multiple):
    return -(-value // multiple) * multiple


class Plan:
    def __init__(self, mesh, pairs):
        dp, leaf = mesh.shape["dp"], mesh.shape["leaf"]
        self.leaf = leaf
        self.devices = dp * leaf
        chip_bits = (dp - 1).bit_length() - 1
        low = (chip_bits + 1) // 2
        x_bits = [leaf << (1 + b) for b in range(low)]
        y_bits = [leaf << (1 + b) for b in range(low, chip_bits)]
        z_bits = [1 << b for b in range((leaf - 1).bit_length())]
        even, odd = [], []
        for b in range(low):
            step = [x_bits[b]] + y_bits[b : b + 1]
            even += step
            odd += step[::-1]
        self.core = leaf
        self.masks = [[leaf] + even + z_bits, [leaf] + odd + z_bits]
        self.steps = len(self.masks[0])
        self.halvings = 0
        while self.halvings < self.steps and pairs >> (self.halvings + 1) << (self.halvings + 1) == pairs:
            self.halvings += 1
        self.pairs = pairs

    def permutation(self, *steps):
        pairs = []
        for device in range(self.devices):
            partner = device
            for step in steps:
                partner ^= self.masks[1 if device & self.core else 0][step]
            pairs.append((device, partner))
        return pairs

    def code(self, device, other):
        odd = (device & self.core) != 0
        codes = []
        for masks in self.masks:
            total = jnp.int32(0)
            for step in range(1, self.halvings):
                half = self.pairs >> (step + 1)
                total = total | jnp.where((device & masks[step]) != 0, half, 0)
            codes.append(total)
        top = self.pairs >> 1
        if other:
            return jnp.where(odd, codes[0], codes[1] | top)
        return jnp.where(odd, codes[1] | top, codes[0])


def own_device(plan):
    return lax.axis_index("dp").astype(jnp.int32) * plan.leaf + lax.axis_index("leaf").astype(jnp.int32)


def one_hot(ids_ref, rows, first, width):
    slot = lax.broadcasted_iota(jnp.int32, (LEAVES, width), 0).astype(jnp.float32).astype(jnp.bfloat16)
    one, zero = jnp.bfloat16(1), jnp.bfloat16(0)
    blocks = []
    for row in rows:
        ids = ids_ref[pl.ds(row, 1), pl.ds(first, width)].astype(jnp.float32).astype(jnp.bfloat16)
        blocks.append(jnp.where(ids == slot, one, zero))
    return jnp.concatenate(blocks, axis=0)


def tree_rows(code, slots):
    rows = []
    for slot in slots:
        first = (slot ^ code) * 2
        rows += [first, first + 1]
    return rows


def groups(slots, size):
    return [slots[i : i + size] for i in range(0, len(slots), size)]


def chunk(rows, limit):
    width = rows
    while width > limit and width % 256 == 0:
        width //= 2
    return width


def pair_sums(hot, stacked):
    return lax.dot_general(hot, stacked, (((1,), (1,)), ((), ())), preferred_element_type=jnp.float32)


def write_sums(sums, out_ref, first):
    classes, half = out_ref.shape[0] // 2, sums.shape[1] // 2
    turned = sums.T
    part = pl.ds(first * PAIR, turned.shape[1])
    out_ref[pl.ds(0, classes), part] = turned[:classes]
    out_ref[pl.ds(classes, classes), part] = turned[half : half + classes]


def add_up(plan, parts, width, stacked_ref, ids_ref, out_refs):
    device = own_device(plan)
    rows = stacked_ref.shape[1]
    todo = []
    for (slots, other), out_ref in zip(parts, out_refs):
        tree = tree_rows(plan.code(device, other), slots)
        todo += [(tree[2 * i : 2 * i + 2], out_ref, i) for i in range(len(slots))]
    for group in groups(todo, 4):
        tree = [row for item in group for row in item[0]]
        total = None
        for first in range(0, rows, width):
            part = pair_sums(one_hot(ids_ref, tree, first, width), stacked_ref[:, first : first + width])
            total = part if total is None else total + part
        for i, (_, out_ref, place) in enumerate(group):
            write_sums(total[i * PAIR : (i + 1) * PAIR], out_ref, place)


def first_kernel(plan, slots, width, predict_hbm, labels_hbm, ids_hbm, stacked_ref, other_ref, ids_ref,
                 predict_ref, labels_ref, sems, ids_sems):
    rows = predict_ref.shape[1]
    classes = predict_ref.shape[0]
    count = rows // width
    size = 2 * len(slots)
    group = tree_rows(plan.code(own_device(plan), True), [slots[0]])[0] & -size
    ids_copies = []
    for i in range(ids_ref.shape[0] // size):
        part = pl.ds(pl.multiple_of(lax.rem(group + i * size, ids_ref.shape[0]), size), size)
        ids_copies.append(pltpu.make_async_copy(ids_hbm.at[part, :], ids_ref.at[part, :], ids_sems.at[i]))
    copies = [pltpu.make_async_copy(labels_hbm, labels_ref, sems.at[0])]
    for i in range(count):
        part = pl.ds(i * width, width)
        copies.append(pltpu.make_async_copy(predict_hbm.at[:, part], predict_ref.at[:, part], sems.at[1 + i]))
    copies[1].start()
    copies[0].start()
    for copy in copies[2:] + ids_copies:
        copy.start()
    copies[0].wait()
    for i in range(count):
        copies[1 + i].wait()
        predict = predict_ref[:, i * width : (i + 1) * width]
        row_max = jnp.max(predict, axis=0, keepdims=True)
        exponent = jnp.exp(predict - row_max)
        probability = exponent * (1.0 / jnp.sum(exponent, axis=0, keepdims=True))
        index = lax.broadcasted_iota(jnp.int32, predict.shape, 0)
        gradient = jnp.where(index == labels_ref[:, i * width : (i + 1) * width], probability - 1.0, probability)
        filler = jnp.zeros((stacked_ref.shape[0] // 2 - classes, width), jnp.float32)
        stacked_ref[:, i * width : (i + 1) * width] = jnp.concatenate(
            [gradient, filler, probability * (1.0 - probability), filler], axis=0
        ).astype(jnp.bfloat16)
    ids_copies[0].wait()
    add_up(plan, [(slots, True)], width, stacked_ref, ids_ref, (other_ref,))
    for copy in ids_copies[1:]:
        copy.wait()


def sums_kernel(plan, parts, width, stacked_ref, ids_ref, _, *out_refs):
    add_up(plan, parts, width, stacked_ref, ids_ref, out_refs)


def sums_cost(count, height, rows):
    return pl.CostEstimate(
        flops=2 * count * PAIR * rows * height, bytes_accessed=2 * height * rows, transcendentals=0
    )


def first_sums(plan, predict, labels, leaf_ids, slots):
    classes, rows = predict.shape
    height = 2 * round_up(classes, 16)
    width = chunk(rows, 1024)
    return pl.pallas_call(
        functools.partial(first_kernel, plan, slots, width),
        in_specs=[IN_HBM, IN_HBM, IN_HBM],
        out_specs=[IN_VMEM, IN_VMEM, IN_VMEM],
        out_shape=[
            pltpu.VMEM((height, rows), jnp.bfloat16),
            pltpu.VMEM((2 * classes, PAIR * len(slots)), jnp.float32),
            pltpu.VMEM(leaf_ids.shape, jnp.int32),
        ],
        scratch_shapes=[
            pltpu.VMEM((classes, rows), jnp.float32),
            pltpu.VMEM((1, rows), jnp.int32),
            pltpu.SemaphoreType.DMA((1 + rows // width,)),
            pltpu.SemaphoreType.DMA((leaf_ids.shape[0] // (2 * len(slots)),)),
        ],
        compiler_params=pltpu.CompilerParams(vmem_limit_bytes=VMEM_LIMIT),
        cost_estimate=sums_cost(len(slots), height, rows),
        name="gradients_and_sums",
    )(*(pltpu.with_memory_space_constraint(x, pltpu.HBM) for x in (predict, labels.reshape(1, rows), leaf_ids)))


def more_sums(plan, stacked, leaf_ids, classes, parts, earlier):
    height, rows = stacked.shape
    return pl.pallas_call(
        functools.partial(sums_kernel, plan, parts, chunk(rows, 2048)),
        in_specs=[IN_VMEM, IN_VMEM, pl.BlockSpec(memory_space=pl.ANY)],
        out_specs=[IN_VMEM] * len(parts),
        out_shape=[jax.ShapeDtypeStruct((2 * classes, PAIR * len(slots)), jnp.float32) for slots, _ in parts],
        compiler_params=pltpu.CompilerParams(vmem_limit_bytes=VMEM_LIMIT),
        cost_estimate=sums_cost(sum(len(slots) for slots, _ in parts), height, rows),
        name="leaf_sums",
    )(stacked, leaf_ids, earlier)


def looked_up(plan, parts, value_refs, ids_ref, first, width):
    device = own_device(plan)
    todo = []
    for (slots, other), value_ref in zip(parts, value_refs):
        tree = tree_rows(plan.code(device, other), slots)
        todo += [(tree[2 * i : 2 * i + 2], value_ref, i) for i in range(len(slots))]
    total = None
    for group in groups(todo, 2):
        tree = [row for item in group for row in item[0]]
        hot = one_hot(ids_ref, tree, first, width)
        values = [ref[:, pl.ds(i * PAIR, PAIR)].astype(jnp.bfloat16) for _, ref, i in group]
        values = values[0] if len(values) == 1 else jnp.concatenate(values, axis=1)
        part = jnp.dot(values, hot, preferred_element_type=jnp.float32)
        total = part if total is None else total + part
    return total


def apply_kernel(plan, parts, width, ids_ref, carried_ref, *refs):
    value_refs, out_ref = refs[:-1], refs[-1]
    for first in range(0, out_ref.shape[1], width):
        part = pl.ds(first, width)
        out_ref[:, part] = carried_ref[:, part] + looked_up(plan, parts, value_refs, ids_ref, first, width)


def apply_cost(count, classes, rows):
    return pl.CostEstimate(
        flops=2 * count * PAIR * rows * 2 * classes, bytes_accessed=4 * classes * rows, transcendentals=0
    )


def apply_values(plan, leaf_ids, parts, values, carried):
    classes, rows = carried.shape
    return pl.pallas_call(
        functools.partial(apply_kernel, plan, parts, chunk(rows, 2048)),
        in_specs=[IN_VMEM] * (2 + len(values)),
        out_specs=IN_VMEM,
        out_shape=jax.ShapeDtypeStruct((classes, rows), jnp.float32),
        compiler_params=pltpu.CompilerParams(vmem_limit_bytes=VMEM_LIMIT),
        cost_estimate=apply_cost(sum(len(slots) for slots, _ in parts), classes, rows),
        name="apply_values",
    )(leaf_ids, carried, *values)


def last_kernel(plan, parts, pieces, width, *refs):
    ids_ref, carried_ref = refs[:2]
    value_refs = refs[2 : 2 + len(pieces)]
    out_hbm, own_hbm, out_ref, own_ref, table_ref, sems = refs[2 + len(pieces) :]
    rows = ids_ref.shape[1]
    count = rows // width
    device = own_device(plan)
    half = plan.pairs // 2
    for (slots, other), value_ref in zip(pieces, value_refs):
        first = slots[0] + (half if other else 0)
        table_ref[:, pl.ds(first * PAIR, len(slots) * PAIR)] = value_ref[...]
    mine, theirs = plan.code(device, False), plan.code(device, True)
    per_leaf = plan.pairs // plan.leaf
    for i in range(per_leaf):
        pair = lax.axis_index("leaf").astype(jnp.int32) * per_leaf + i
        place = pair ^ mine
        place = jnp.where(place < half, place, (pair ^ theirs) + half)
        own_ref[:, pl.ds(i * PAIR, PAIR)] = table_ref[:, pl.ds(pl.multiple_of(place * PAIR, PAIR), PAIR)]
    writes = []
    last = [value_refs[pieces.index(piece)] for piece in parts]
    for i in range(count):
        part = pl.ds(i * width, width)
        out_ref[:, part] = carried_ref[:, part] + looked_up(plan, parts, last, ids_ref, i * width, width)
        writes.append(pltpu.make_async_copy(out_ref.at[:, part], out_hbm.at[:, part], sems.at[i]))
        writes[-1].start()
        if i == 0:
            writes.append(pltpu.make_async_copy(own_ref, own_hbm, sems.at[count]))
            writes[-1].start()
    for write in writes:
        write.wait()


def finish(plan, leaf_ids, carried, parts, pieces, values):
    classes, rows = carried.shape
    width = chunk(rows, 1024)
    own = (classes, plan.pairs // plan.leaf * PAIR)
    return pl.pallas_call(
        functools.partial(last_kernel, plan, parts, pieces, width),
        in_specs=[IN_VMEM] * (2 + len(values)),
        out_specs=[IN_HBM, IN_HBM],
        out_shape=[jax.ShapeDtypeStruct((classes, rows), jnp.float32), jax.ShapeDtypeStruct(own, jnp.float32)],
        scratch_shapes=[
            pltpu.VMEM((classes, rows), jnp.float32),
            pltpu.VMEM(own, jnp.float32),
            pltpu.VMEM((classes, plan.pairs * PAIR), jnp.float32),
            pltpu.SemaphoreType.DMA((rows // width + 1,)),
        ],
        compiler_params=pltpu.CompilerParams(vmem_limit_bytes=VMEM_LIMIT),
        cost_estimate=apply_cost(sum(len(slots) for slots, _ in parts), classes, rows),
        name="apply_last_values",
    )(leaf_ids, carried, *values)


def newton(sums):
    classes = sums.shape[0] // 2
    return -STEP_SIZE * sums[:classes] / (sums[classes:] + RIDGE_TERM)


def solution(mesh):
    def shards(predict, labels, leaf_ids):
        classes = predict.shape[0]
        plan = Plan(mesh, leaf_ids.shape[0] // 2)

        def exchange(value, *steps):
            return lax.ppermute(value, AXES, plan.permutation(*steps))

        h = plan.pairs // 2
        unit = h // 8
        far = list(range(h // 2, h))
        near = list(range(h // 2))
        own, by_3, by_2, by_both = (near[i * unit : (i + 1) * unit] for i in range(4))

        stacked, far_other, leaf_ids = first_sums(plan, predict, labels, leaf_ids, far)
        (far_own,) = more_sums(plan, stacked, leaf_ids, classes, [(far, False)], far_other)
        far_sums = far_own + exchange(far_other, 0)
        far_moved = exchange(far_sums, 1)
        near_other, upper_own = more_sums(
            plan, stacked, leaf_ids, classes, [(near, True), (by_2 + by_both, False)], far_sums
        )
        near_core = exchange(near_other, 0)
        (lower_own,) = more_sums(plan, stacked, leaf_ids, classes, [(own + by_3, False)], near_other)

        def quarter(i):
            part = slice(PAIR * unit * i, PAIR * unit * (i + 1))
            inner = slice(PAIR * unit * (i % 2), PAIR * unit * (i % 2 + 1))
            return (upper_own if i > 1 else lower_own)[:, inner] + near_core[:, part] + far_moved[:, part]

        held = quarter(0)
        held = held + exchange(quarter(3), 2, 3) + exchange(quarter(1), 3) + exchange(quarter(2), 2)
        for step in range(4, plan.steps):
            if step < plan.halvings:
                keep = held.shape[1] // 2
                held = held[:, :keep] + exchange(held[:, keep:], step)
            else:
                held = held + exchange(held, step)
        values = newton(held)
        for step in reversed(range(4, plan.halvings)):
            values = jnp.concatenate([values, exchange(values, step)], axis=1)

        moved = [exchange(values, 3), exchange(values, 2), exchange(values, 2, 3)]
        near_values = jnp.concatenate([values] + moved, axis=1)
        far_values = exchange(near_values, 1)
        near_theirs = exchange(near_values, 0)
        update = apply_values(
            plan, leaf_ids, [(near, False), (near, True)], [near_values, near_theirs], predict
        )
        far_values, update = lax.optimization_barrier((far_values, update))
        far_theirs = exchange(far_values, 0)
        update = apply_values(plan, leaf_ids, [(far, False)], [far_values], update)
        pieces = [(near, False), (far, False), (near, True), (far, True)]
        values = [near_values, far_values, near_theirs, far_theirs]
        return tuple(finish(plan, leaf_ids, update, [(far, True)], pieces, values))

    return jax.shard_map(
        shards,
        mesh=mesh,
        in_specs=(P(None, AXES), P(AXES), P(None, AXES)),
        out_specs=(P(None, AXES), P(None, "leaf")),
        check_vma=False,
    )
```

```python
import functools

import jax
import jax.numpy as jnp
from jax import lax
from jax.experimental import pallas as pl
from jax.experimental.pallas import tpu as pltpu
from jax.sharding import PartitionSpec as P

LEAVES = 64
PAIR = 2 * LEAVES
STEP_SIZE = 0.5
RIDGE_TERM = 1.0
VMEM_LIMIT = 24 * 1024 * 1024
AXES = ("dp", "leaf")
IN_VMEM = pl.BlockSpec(memory_space=pltpu.VMEM)
IN_HBM = pl.BlockSpec(memory_space=pltpu.HBM)


def round_up(value, multiple):
    return -(-value // multiple) * multiple


class Plan:
    def __init__(self, mesh, pairs):
        dp, leaf = mesh.shape["dp"], mesh.shape["leaf"]
        self.leaf = leaf
        self.devices = dp * leaf
        chip_bits = (dp - 1).bit_length() - 1
        low = (chip_bits + 1) // 2
        x_bits = [leaf << (1 + b) for b in range(low)]
        y_bits = [leaf << (1 + b) for b in range(low, chip_bits)]
        z_bits = [1 << b for b in range((leaf - 1).bit_length())]
        even, odd = [], []
        for b in range(low):
            step = [x_bits[b]] + y_bits[b : b + 1]
            even += step
            odd += step[::-1]
        self.core = leaf
        self.masks = [[leaf] + even + z_bits, [leaf] + odd + z_bits]
        self.steps = len(self.masks[0])
        self.halvings = 0
        while self.halvings < self.steps and pairs >> (self.halvings + 1) << (self.halvings + 1) == pairs:
            self.halvings += 1
        self.pairs = pairs

    def permutation(self, *steps):
        pairs = []
        for device in range(self.devices):
            partner = device
            for step in steps:
                partner ^= self.masks[1 if device & self.core else 0][step]
            pairs.append((device, partner))
        return pairs

    def code(self, device, other):
        odd = (device & self.core) != 0
        codes = []
        for masks in self.masks:
            total = jnp.int32(0)
            for step in range(1, self.halvings):
                half = self.pairs >> (step + 1)
                total = total | jnp.where((device & masks[step]) != 0, half, 0)
            codes.append(total)
        top = self.pairs >> 1
        if other:
            return jnp.where(odd, codes[0], codes[1] | top)
        return jnp.where(odd, codes[1] | top, codes[0])


def own_device(plan):
    return lax.axis_index("dp").astype(jnp.int32) * plan.leaf + lax.axis_index("leaf").astype(jnp.int32)


def one_hot(ids_ref, rows, first, width):
    slot = lax.broadcasted_iota(jnp.int32, (LEAVES, width), 0).astype(jnp.float32).astype(jnp.bfloat16)
    one, zero = jnp.bfloat16(1), jnp.bfloat16(0)
    blocks = []
    for row in rows:
        ids = ids_ref[pl.ds(row, 1), pl.ds(first, width)].astype(jnp.float32).astype(jnp.bfloat16)
        blocks.append(jnp.where(ids == slot, one, zero))
    return jnp.concatenate(blocks, axis=0)


def tree_rows(code, slots):
    rows = []
    for slot in slots:
        first = (slot ^ code) * 2
        rows += [first, first + 1]
    return rows


def groups(slots, size):
    return [slots[i : i + size] for i in range(0, len(slots), size)]


def chunk(rows, limit):
    width = rows
    while width > limit and width % 256 == 0:
        width //= 2
    return width


def pair_sums(hot, stacked):
    return lax.dot_general(hot, stacked, (((1,), (1,)), ((), ())), preferred_element_type=jnp.float32)


def write_sums(sums, out_ref, first):
    classes, half = out_ref.shape[0] // 2, sums.shape[1] // 2
    turned = sums.T
    part = pl.ds(first * PAIR, turned.shape[1])
    out_ref[pl.ds(0, classes), part] = turned[:classes]
    out_ref[pl.ds(classes, classes), part] = turned[half : half + classes]


def add_up(plan, parts, width, stacked_ref, ids_ref, out_refs):
    device = own_device(plan)
    rows = stacked_ref.shape[1]
    todo = []
    for (slots, other), out_ref in zip(parts, out_refs):
        tree = tree_rows(plan.code(device, other), slots)
        todo += [(tree[2 * i : 2 * i + 2], out_ref, i) for i in range(len(slots))]
    for group in groups(todo, 4):
        tree = [row for item in group for row in item[0]]
        total = None
        for first in range(0, rows, width):
            part = pair_sums(one_hot(ids_ref, tree, first, width), stacked_ref[:, first : first + width])
            total = part if total is None else total + part
        for i, (_, out_ref, place) in enumerate(group):
            write_sums(total[i * PAIR : (i + 1) * PAIR], out_ref, place)


def first_kernel(plan, slots, width, predict_hbm, labels_hbm, ids_hbm, stacked_ref, other_ref, ids_ref,
                 predict_ref, labels_ref, sems, ids_sems):
    rows = predict_ref.shape[1]
    classes = predict_ref.shape[0]
    count = rows // width
    size = 2 * len(slots)
    group = tree_rows(plan.code(own_device(plan), True), [slots[0]])[0] & -size
    ids_copies = []
    for i in range(ids_ref.shape[0] // size):
        part = pl.ds(pl.multiple_of(lax.rem(group + i * size, ids_ref.shape[0]), size), size)
        ids_copies.append(pltpu.make_async_copy(ids_hbm.at[part, :], ids_ref.at[part, :], ids_sems.at[i]))
    copies = [pltpu.make_async_copy(labels_hbm, labels_ref, sems.at[0])]
    for i in range(count):
        part = pl.ds(i * width, width)
        copies.append(pltpu.make_async_copy(predict_hbm.at[:, part], predict_ref.at[:, part], sems.at[1 + i]))
    copies[1].start()
    copies[0].start()
    for copy in copies[2:] + ids_copies:
        copy.start()
    copies[0].wait()
    for i in range(count):
        copies[1 + i].wait()
        predict = predict_ref[:, i * width : (i + 1) * width]
        row_max = jnp.max(predict, axis=0, keepdims=True)
        exponent = jnp.exp(predict - row_max)
        probability = exponent * (1.0 / jnp.sum(exponent, axis=0, keepdims=True))
        index = lax.broadcasted_iota(jnp.int32, predict.shape, 0)
        gradient = jnp.where(index == labels_ref[:, i * width : (i + 1) * width], probability - 1.0, probability)
        filler = jnp.zeros((stacked_ref.shape[0] // 2 - classes, width), jnp.float32)
        stacked_ref[:, i * width : (i + 1) * width] = jnp.concatenate(
            [gradient, filler, probability * (1.0 - probability), filler], axis=0
        ).astype(jnp.bfloat16)
    ids_copies[0].wait()
    add_up(plan, [(slots, True)], width, stacked_ref, ids_ref, (other_ref,))
    for copy in ids_copies[1:]:
        copy.wait()


def sums_kernel(plan, parts, width, stacked_ref, ids_ref, _, *out_refs):
    add_up(plan, parts, width, stacked_ref, ids_ref, out_refs)


def sums_cost(count, height, rows):
    return pl.CostEstimate(
        flops=2 * count * PAIR * rows * height, bytes_accessed=2 * height * rows, transcendentals=0
    )


def first_sums(plan, predict, labels, leaf_ids, slots):
    classes, rows = predict.shape
    height = 2 * round_up(classes, 16)
    width = chunk(rows, 1024)
    return pl.pallas_call(
        functools.partial(first_kernel, plan, slots, width),
        in_specs=[IN_HBM, IN_HBM, IN_HBM],
        out_specs=[IN_VMEM, IN_VMEM, IN_VMEM],
        out_shape=[
            pltpu.VMEM((height, rows), jnp.bfloat16),
            pltpu.VMEM((2 * classes, PAIR * len(slots)), jnp.float32),
            pltpu.VMEM(leaf_ids.shape, jnp.int32),
        ],
        scratch_shapes=[
            pltpu.VMEM((classes, rows), jnp.float32),
            pltpu.VMEM((1, rows), jnp.int32),
            pltpu.SemaphoreType.DMA((1 + rows // width,)),
            pltpu.SemaphoreType.DMA((leaf_ids.shape[0] // (2 * len(slots)),)),
        ],
        compiler_params=pltpu.CompilerParams(vmem_limit_bytes=VMEM_LIMIT),
        cost_estimate=sums_cost(len(slots), height, rows),
        name="gradients_and_sums",
    )(*(pltpu.with_memory_space_constraint(x, pltpu.HBM) for x in (predict, labels.reshape(1, rows), leaf_ids)))


def more_sums(plan, stacked, leaf_ids, classes, parts, earlier):
    height, rows = stacked.shape
    return pl.pallas_call(
        functools.partial(sums_kernel, plan, parts, chunk(rows, 2048)),
        in_specs=[IN_VMEM, IN_VMEM, pl.BlockSpec(memory_space=pl.ANY)],
        out_specs=[IN_VMEM] * len(parts),
        out_shape=[jax.ShapeDtypeStruct((2 * classes, PAIR * len(slots)), jnp.float32) for slots, _ in parts],
        compiler_params=pltpu.CompilerParams(vmem_limit_bytes=VMEM_LIMIT),
        cost_estimate=sums_cost(sum(len(slots) for slots, _ in parts), height, rows),
        name="leaf_sums",
    )(stacked, leaf_ids, earlier)


def looked_up(plan, parts, value_refs, ids_ref, first, width):
    device = own_device(plan)
    todo = []
    for (slots, other), value_ref in zip(parts, value_refs):
        tree = tree_rows(plan.code(device, other), slots)
        todo += [(tree[2 * i : 2 * i + 2], value_ref, i) for i in range(len(slots))]
    total = None
    for group in groups(todo, 2):
        tree = [row for item in group for row in item[0]]
        hot = one_hot(ids_ref, tree, first, width)
        values = [ref[:, pl.ds(i * PAIR, PAIR)].astype(jnp.bfloat16) for _, ref, i in group]
        values = values[0] if len(values) == 1 else jnp.concatenate(values, axis=1)
        part = jnp.dot(values, hot, preferred_element_type=jnp.float32)
        total = part if total is None else total + part
    return total


def apply_kernel(plan, parts, width, ids_ref, carried_ref, *refs):
    value_refs, out_ref = refs[:-1], refs[-1]
    for first in range(0, out_ref.shape[1], width):
        part = pl.ds(first, width)
        out_ref[:, part] = carried_ref[:, part] + looked_up(plan, parts, value_refs, ids_ref, first, width)


def apply_cost(count, classes, rows):
    return pl.CostEstimate(
        flops=2 * count * PAIR * rows * 2 * classes, bytes_accessed=4 * classes * rows, transcendentals=0
    )


def apply_values(plan, leaf_ids, parts, values, carried):
    classes, rows = carried.shape
    return pl.pallas_call(
        functools.partial(apply_kernel, plan, parts, chunk(rows, 2048)),
        in_specs=[IN_VMEM] * (2 + len(values)),
        out_specs=IN_VMEM,
        out_shape=jax.ShapeDtypeStruct((classes, rows), jnp.float32),
        compiler_params=pltpu.CompilerParams(vmem_limit_bytes=VMEM_LIMIT),
        cost_estimate=apply_cost(sum(len(slots) for slots, _ in parts), classes, rows),
        name="apply_values",
    )(leaf_ids, carried, *values)


def last_kernel(plan, parts, pieces, width, *refs):
    ids_ref, carried_ref = refs[:2]
    value_refs = refs[2 : 2 + len(pieces)]
    out_hbm, own_hbm, out_ref, own_ref, sems = refs[2 + len(pieces) :]
    rows = ids_ref.shape[1]
    count = rows // width
    device = own_device(plan)
    half = plan.pairs // 2
    mine, theirs = plan.code(device, False), plan.code(device, True)
    per_leaf = plan.pairs // plan.leaf
    for i in range(per_leaf):
        pair = lax.axis_index("leaf").astype(jnp.int32) * per_leaf + i
        place = pair ^ mine
        place = jnp.where(place < half, place, (pair ^ theirs) + half)
        picked = None
        for (slots, other), value_ref in zip(pieces, value_refs):
            offset = place - (slots[0] + (half if other else 0))
            inside = jnp.clip(offset, 0, len(slots) - 1)
            block = value_ref[:, pl.ds(pl.multiple_of(inside * PAIR, PAIR), PAIR)]
            picked = block if picked is None else jnp.where(offset == inside, block, picked)
        own_ref[:, pl.ds(i * PAIR, PAIR)] = picked
    writes = []
    last = [value_refs[pieces.index(piece)] for piece in parts]
    for i in range(count):
        part = pl.ds(i * width, width)
        out_ref[:, part] = carried_ref[:, part] + looked_up(plan, parts, last, ids_ref, i * width, width)
        writes.append(pltpu.make_async_copy(out_ref.at[:, part], out_hbm.at[:, part], sems.at[i]))
        writes[-1].start()
        if i == 0:
            writes.append(pltpu.make_async_copy(own_ref, own_hbm, sems.at[count]))
            writes[-1].start()
    for write in writes:
        write.wait()


def finish(plan, leaf_ids, carried, parts, pieces, values):
    classes, rows = carried.shape
    width = chunk(rows, 1024)
    own = (classes, plan.pairs // plan.leaf * PAIR)
    return pl.pallas_call(
        functools.partial(last_kernel, plan, parts, pieces, width),
        in_specs=[IN_VMEM] * (2 + len(values)),
        out_specs=[IN_HBM, IN_HBM],
        out_shape=[jax.ShapeDtypeStruct((classes, rows), jnp.float32), jax.ShapeDtypeStruct(own, jnp.float32)],
        scratch_shapes=[
            pltpu.VMEM((classes, rows), jnp.float32),
            pltpu.VMEM(own, jnp.float32),
            pltpu.SemaphoreType.DMA((rows // width + 1,)),
        ],
        compiler_params=pltpu.CompilerParams(vmem_limit_bytes=VMEM_LIMIT),
        cost_estimate=apply_cost(sum(len(slots) for slots, _ in parts), classes, rows),
        name="apply_last_values",
    )(leaf_ids, carried, *values)


def newton(sums):
    classes = sums.shape[0] // 2
    return -STEP_SIZE * sums[:classes] / (sums[classes:] + RIDGE_TERM)


def solution(mesh):
    def shards(predict, labels, leaf_ids):
        classes = predict.shape[0]
        plan = Plan(mesh, leaf_ids.shape[0] // 2)

        def exchange(value, *steps):
            return lax.ppermute(value, AXES, plan.permutation(*steps))

        h = plan.pairs // 2
        unit = h // 8
        far = list(range(h // 2, h))
        near = list(range(h // 2))
        own, by_3, by_2, by_both = (near[i * unit : (i + 1) * unit] for i in range(4))

        stacked, far_other, leaf_ids = first_sums(plan, predict, labels, leaf_ids, far)
        (far_own,) = more_sums(plan, stacked, leaf_ids, classes, [(far, False)], far_other)
        far_sums = far_own + exchange(far_other, 0)
        far_moved = exchange(far_sums, 1)
        near_other, upper_own = more_sums(
            plan, stacked, leaf_ids, classes, [(near, True), (by_2 + by_both, False)], far_sums
        )
        near_core = exchange(near_other, 0)
        (lower_own,) = more_sums(plan, stacked, leaf_ids, classes, [(own + by_3, False)], near_other)

        def quarter(i):
            part = slice(PAIR * unit * i, PAIR * unit * (i + 1))
            inner = slice(PAIR * unit * (i % 2), PAIR * unit * (i % 2 + 1))
            return (upper_own if i > 1 else lower_own)[:, inner] + near_core[:, part] + far_moved[:, part]

        held = quarter(0)
        held = held + exchange(quarter(3), 2, 3) + exchange(quarter(1), 3) + exchange(quarter(2), 2)
        for step in range(4, plan.steps):
            if step < plan.halvings:
                keep = held.shape[1] // 2
                held = held[:, :keep] + exchange(held[:, keep:], step)
            else:
                held = held + exchange(held, step)
        values = newton(held)
        for step in reversed(range(4, plan.halvings)):
            values = jnp.concatenate([values, exchange(values, step)], axis=1)

        moved = [exchange(values, 3), exchange(values, 2), exchange(values, 2, 3)]
        near_values = jnp.concatenate([values] + moved, axis=1)
        far_values = exchange(near_values, 1)
        near_theirs = exchange(near_values, 0)
        update = apply_values(
            plan, leaf_ids, [(near, False), (near, True)], [near_values, near_theirs], predict
        )
        far_values, update = lax.optimization_barrier((far_values, update))
        far_theirs = exchange(far_values, 0)
        update = apply_values(plan, leaf_ids, [(far, False)], [far_values], update)
        pieces = [(near, False), (far, False), (near, True), (far, True)]
        values = [near_values, far_values, near_theirs, far_theirs]
        return tuple(finish(plan, leaf_ids, update, [(far, True)], pieces, values))

    return jax.shard_map(
        shards,
        mesh=mesh,
        in_specs=(P(None, AXES), P(AXES), P(None, AXES)),
        out_specs=(P(None, AXES), P(None, "leaf")),
        check_vma=False,
    )
```
